512 devices in a mesh: dom: 32 (over x, z), member: 16 (over y, core).
Axes of the slice: x: 4, y: 8, z: 8, core: 2. Of those that a mesh axis runs over, the one named last changes fastest.
Arguments:
- features: bfloat16 [131072, 256], P(('dom', 'member')), may hold values from -6 to 6
- cotangent: bfloat16 [131072, 256], P(('dom', 'member')), may hold values from -6 to 6
- edge_src: int32 [32, 16, 4096], P('dom', 'member'), may hold values from -1 to 4095, as said below
- edge_dst: int32 [32, 16, 4096], P('dom', 'member'), may hold values from -1 to 4095, as said below
- send_rows: int32 [32, 16, 32, 4], P('dom', 'member'), may hold values from -1 to 255, as said below
- recv_rows: int32 [32, 16, 32, 4], P('dom', 'member'), may hold values from -1 to 193, as said below
- in_degree: int32 [32, 16, 256], P('dom', 'member'), may hold values from 0 to 2097168, as said below
- weight_self: bfloat16 [256, 256], replicated, may hold values from -0.375 to 0.375
- weight_neigh: bfloat16 [256, 256], replicated, may hold values from -0.375 to 0.375
Outputs:
- activated: bfloat16 [131072, 256], P(('dom', 'member'))
- grad_features: bfloat16 [131072, 256], P(('dom', 'member'))
- grad_self: float32 [256, 256], replicated
- grad_neigh: float32 [256, 256], replicated
The draws below stay inside these ranges and needn't reach their ends.
Inputs may be any that keep to these rules, and one draw needn't show every extreme that they name: Live edge slots of a device form a prefix; edge_src and edge_dst are -1 together exactly on the padding. Some device of every partition has all 4096 slots live. `edge_dst`: same padding as edge_src. `send_rows`: each of a device's 62 mirror rows (its last 62 rows) appears in exactly one slot; no slot to the device's own partition; at most 4 slots to one peer, and exactly 4 to some peer of every device. recv_rows[q, m, p, k] >= 0 exactly where send_rows[p, m, q, k] >= 0; it names a master row (below 194), distinct over k for one q, m, p. `in_degree`: equal at all replicas of a vertex.
All inputs are finite; a program needn't handle non-finite values.
Results may differ from the reference program's by a relative error of at most 0.018.
Values may be sent and summed in bfloat16 or wider, within the bound.
No kernel may reach another device: no remote copies, remote signals or barrier semaphores. Data moves between devices by JAX's collectives and lax.ppermute only.
A program may use at most 64 MiB of HBM per device.

```python
import jax
import jax.numpy as jnp
from jax import lax

F = 256
RM = 256
E_DEV = 4096
CAP = 4
MIRR = 62
R = 4096
TOTAL = 131072
N_DOM = 32
N_MEMBER = 16


def graph_layout(key):
    streams = jax.random.split(key, 10)
    devices_all = N_DOM * N_MEMBER
    slot_total = (N_DOM - 1) * CAP
    master_count = RM - MIRR
    part_rows = N_MEMBER * RM
    total_rows = N_DOM * part_rows
    device_ids = jnp.arange(devices_all, dtype=jnp.int32)
    dom_of = device_ids // N_MEMBER
    member_of = device_ids % N_MEMBER
    slot_ids = jnp.arange(slot_total, dtype=jnp.int32)
    scores = jax.vmap(lambda stream: jax.random.permutation(stream, slot_total))(jax.random.split(streams[0], devices_all)).astype(jnp.int32)
    favored = jax.random.randint(streams[1], (devices_all, 1), 0, N_DOM - 1)
    scores = jnp.where(slot_ids[None, :] // CAP == favored, -1 - slot_ids[None, :] % CAP, scores)
    chosen = jnp.argsort(scores, axis=1, stable=True)[:, :MIRR].astype(jnp.int32)
    target = (dom_of[:, None] + 1 + chosen // CAP) % N_DOM
    within = chosen % CAP
    mirror_rows = jnp.broadcast_to(RM - MIRR + jnp.arange(MIRR, dtype=jnp.int32), (devices_all, MIRR))
    sender = jnp.broadcast_to(device_ids[:, None], (devices_all, MIRR))
    send_rows = jnp.full((devices_all, N_DOM, CAP), -1, jnp.int32).at[sender, target, within].set(mirror_rows)
    send_rows = send_rows.reshape(N_DOM, N_MEMBER, N_DOM, CAP)
    offsets = jax.random.randint(streams[2], (N_DOM, N_MEMBER, N_DOM, 1), 0, master_count)
    first_peer = (1 + favored[0, 0]) % N_DOM
    offsets = offsets.at[first_peer, 0, 0, 0].set(master_count - CAP)
    landing = (offsets + jnp.arange(CAP, dtype=jnp.int32)) % master_count
    recv_rows = jnp.where(jnp.transpose(send_rows, (2, 1, 0, 3)) >= 0, landing, -1).astype(jnp.int32)
    extra = jax.random.randint(streams[3], (devices_all,), 0, 3 * E_DEV // 4 + 1)
    live = jnp.where(member_of == dom_of % N_MEMBER, E_DEV, E_DEV // 4 + extra)
    sources = jax.random.randint(streams[4], (devices_all, E_DEV), 0, part_rows)
    sources = sources.at[:, 0].set(part_rows - 1)
    hot_rows = jax.random.randint(streams[5], (N_DOM, 8), 0, part_rows)
    coins = jax.random.randint(streams[6], (devices_all, E_DEV), 0, 4)
    picks = jax.random.randint(streams[7], (devices_all, E_DEV), 0, 8)
    spread_rows = jax.random.randint(streams[8], (devices_all, E_DEV), 0, part_rows)
    hot_dest = jnp.take_along_axis(hot_rows[dom_of], picks, axis=1)
    dest_rows = jnp.where(coins == 0, hot_dest, spread_rows)
    dest_rows = dest_rows.at[:, 1].set(part_rows - 1)
    usable = jnp.arange(E_DEV, dtype=jnp.int32)[None, :] < live[:, None]
    edge_src = jnp.where(usable, sources, -1).astype(jnp.int32).reshape(N_DOM, N_MEMBER, E_DEV)
    edge_dst = jnp.where(usable, dest_rows, -1).astype(jnp.int32).reshape(N_DOM, N_MEMBER, E_DEV)
    flat_dest = jnp.where(usable, dom_of[:, None] * part_rows + dest_rows, total_rows)
    counts = jnp.zeros((total_rows + 1,), jnp.int32).at[flat_dest.reshape(-1)].add(1)[:total_rows]
    layout_shape = send_rows.shape
    dom_index = lax.broadcasted_iota(jnp.int32, layout_shape, 0)
    member_index = lax.broadcasted_iota(jnp.int32, layout_shape, 1)
    peer_index = lax.broadcasted_iota(jnp.int32, layout_shape, 2)
    landing_back = jnp.transpose(recv_rows, (2, 1, 0, 3))
    mirror_at = jnp.where(send_rows >= 0, dom_index * part_rows + member_index * RM + send_rows, total_rows)
    master_at = peer_index * part_rows + member_index * RM + landing_back
    own_rows = jnp.arange(total_rows, dtype=jnp.int32)
    owners = own_rows.at[mirror_at.reshape(-1)].set(master_at.reshape(-1), mode='drop')
    vertex_counts = jax.ops.segment_sum(counts, owners, num_segments=total_rows)
    outside = jax.random.randint(streams[9], (total_rows,), 0, 16)
    top_degree = devices_all * E_DEV + 16
    outside = outside.at[0].set(top_degree - vertex_counts[0])
    in_degree = (vertex_counts + outside)[owners].astype(jnp.int32).reshape(N_DOM, N_MEMBER, RM)
    return (edge_src, edge_dst, send_rows, recv_rows, in_degree)


def draw_edge_src(key, part):
    return graph_layout(key)[0]


def draw_edge_dst(key, part):
    return graph_layout(key)[1]


def draw_send_rows(key, part):
    return graph_layout(key)[2]


def draw_recv_rows(key, part):
    return graph_layout(key)[3]


def draw_in_degree(key, part):
    return graph_layout(key)[4]


def shard_levels(rng, extent, cuts, least, high):
    level, own = 1.0, jax.random.fold_in(rng, 6)
    for axis_at, parts in cuts:
        draws = jnp.exp(jax.random.uniform(jax.random.fold_in(own, axis_at), (parts,), jnp.float32, least / len(cuts), high / len(cuts)))
        level = level * jnp.repeat(draws, extent[axis_at] // parts).reshape([-1 if axis == axis_at else 1 for axis in range(len(extent))])
    return level


def scatter_about(rng, extent, scale, most, cuts=(), held_as=jnp.bfloat16):
    entries = scale * jax.random.normal(rng, extent, jnp.float32)
    if cuts:
        entries = entries * shard_levels(rng, extent, cuts, -0.22, 0.18)
    return jnp.clip(entries, -most, most).astype(held_as)


def setup_inputs(seed: int = 0) -> dict:
    streams_of = jax.random.split(jax.random.key(seed), 10)
    return {
        "features": scatter_about(streams_of[0], (TOTAL, F), 1.0, 6.0, ((0, 512),)),
        "cotangent": scatter_about(streams_of[1], (TOTAL, F), 1.0, 6.0, ((0, 512),)),
        "edge_src": draw_edge_src(jax.random.fold_in(streams_of[9], 71), 0),
        "edge_dst": draw_edge_dst(jax.random.fold_in(streams_of[9], 71), 0),
        "send_rows": draw_send_rows(jax.random.fold_in(streams_of[9], 71), 0),
        "recv_rows": draw_recv_rows(jax.random.fold_in(streams_of[9], 71), 0),
        "in_degree": draw_in_degree(jax.random.fold_in(streams_of[9], 71), 0),
        "weight_self": scatter_about(streams_of[7], (F, F), F ** -0.5, 0.375),
        "weight_neigh": scatter_about(streams_of[8], (F, F), F ** -0.5, 0.375),
    }


def rounded(values):
    return lax.optimization_barrier(values.astype(jnp.bfloat16)).astype(jnp.float32)


def owner_map(send_rows, recv_rows):
    layout_shape = send_rows.shape
    dom_index = lax.broadcasted_iota(jnp.int32, layout_shape, 0)
    member_index = lax.broadcasted_iota(jnp.int32, layout_shape, 1)
    peer_index = lax.broadcasted_iota(jnp.int32, layout_shape, 2)
    landing = jnp.transpose(recv_rows, (2, 1, 0, 3))
    mirror_at = jnp.where(send_rows >= 0, dom_index * R + member_index * RM + send_rows, TOTAL).astype(jnp.int32)
    master_at = (peer_index * R + member_index * RM + landing).astype(jnp.int32)
    own_rows = jnp.arange(TOTAL, dtype=jnp.int32)
    owners = own_rows.at[mirror_at.reshape(-1)].set(master_at.reshape(-1), mode="drop")
    return owners, owners == own_rows


def device_partial(source_table, take_rows, place_rows):
    usable = take_rows >= 0
    messages = jnp.where(usable[:, None], source_table[jnp.where(usable, take_rows, 0)].astype(jnp.float32), 0.0)
    partial_rows = jax.ops.segment_sum(messages, jnp.where(usable, place_rows, R), num_segments=R + 1)[:R]
    return rounded(partial_rows)


def partition_sums(table_all, take_all, place_all):
    def one_partition(operands):
        source_table, take_block, place_block = operands
        per_member = jax.vmap(lambda take_rows, place_rows: device_partial(source_table, take_rows, place_rows))(take_block, place_block)
        return jnp.sum(per_member, axis=0)
    width_now = table_all.shape[1]
    return lax.map(one_partition, (table_all.reshape(N_DOM, R, width_now), take_all, place_all)).reshape(TOTAL, width_now)


def reference(features, cotangent, edge_src, edge_dst, send_rows, recv_rows, in_degree, weight_self, weight_neigh):
    owners, is_master = owner_map(send_rows, recv_rows)
    master_col = is_master[:, None]
    denominator = in_degree.reshape(TOTAL).astype(jnp.float32)[:, None] + 1.0
    pulled = features[owners]
    member_total = partition_sums(pulled, edge_src, edge_dst)
    totals = jax.ops.segment_sum(jnp.where(master_col, member_total, rounded(member_total)), owners, num_segments=TOTAL)
    averaged = (totals / denominator).astype(jnp.bfloat16)[owners]
    pre = jnp.dot(pulled, weight_self, preferred_element_type=jnp.float32) + jnp.dot(averaged, weight_neigh, preferred_element_type=jnp.float32)
    gate_sig = jax.nn.sigmoid(pre)
    activated = (pre * gate_sig).astype(jnp.bfloat16)
    slope = gate_sig * (1.0 + pre * (1.0 - gate_sig))
    grad_pre = jnp.where(master_col, cotangent.astype(jnp.float32) * slope, 0.0).astype(jnp.bfloat16)
    grad_self = jnp.dot(pulled.T, grad_pre, preferred_element_type=jnp.float32)
    grad_neigh = jnp.dot(averaged.T, grad_pre, preferred_element_type=jnp.float32)
    grad_mean = (jnp.dot(grad_pre, weight_neigh.T, preferred_element_type=jnp.float32) / denominator).astype(jnp.bfloat16)[owners]
    back_total = partition_sums(grad_mean, edge_dst, edge_src)
    back_sum = jax.ops.segment_sum(jnp.where(master_col, back_total, rounded(back_total)), owners, num_segments=TOTAL)
    self_term = jnp.dot(grad_pre, weight_self.T, preferred_element_type=jnp.float32)
    grad_features = jnp.where(master_col, back_sum + self_term, 0.0).astype(jnp.bfloat16)
    return activated, grad_features, grad_self, grad_neigh
```

```python
import functools

import jax
import jax.numpy as jnp
from jax import lax
from jax.experimental import pallas as pl
from jax.experimental.pallas import tpu as pltpu
from jax.sharding import Mesh, PartitionSpec as P

MIRR = 62
LATE = 64
UNROLL = 16
ACCS = 4
CHUNK = 128


def edge_kernel(
    take_high, counts_ref, packed_ref, early_ref, late_ref, early_out, late_out, table, *accs
):
    early_rows, late_rows = early_ref.shape[0], late_ref.shape[0]
    rows = early_rows + late_rows
    pad = table.shape[0] - rows

    def load(ref, base):
        def step(i, _):
            at = pl.multiple_of(i * CHUNK, CHUNK)
            table[pl.ds(base + at, CHUNK), :] = ref[pl.ds(at, CHUNK), :].astype(jnp.float32)
            for acc in accs:
                acc[pl.ds(base + at, CHUNK), :] = jnp.zeros((CHUNK, ref.shape[1]), jnp.float32)
            return 0

        lax.fori_loop(0, ref.shape[0] // CHUNK, step, 0)

    load(early_ref, 0)
    load(late_ref, early_rows)
    table[pl.ds(rows, pad), :] = jnp.zeros((pad, table.shape[1]), jnp.float32)

    for which in range(2):

        def step(i, _):
            for group in range(UNROLL // ACCS):
                takes, places = [], []
                for k in range(ACCS):
                    word = packed_ref[which, i * UNROLL + group * ACCS + k]
                    low, high = word & 0xFFFF, word >> 16
                    takes.append(high if take_high else low)
                    places.append(low if take_high else high)
                sums = [
                    accs[k][pl.ds(places[k], 1), :] + table[pl.ds(takes[k], 1), :]
                    for k in range(ACCS)
                ]
                for k in range(ACCS):
                    accs[k][pl.ds(places[k], 1), :] = sums[k]
            return 0

        lax.fori_loop(0, counts_ref[which], step, 0)

    def store(ref, base):
        def step(i, _):
            at = pl.multiple_of(i * CHUNK, CHUNK)
            total = accs[0][pl.ds(base + at, CHUNK), :]
            for acc in accs[1:]:
                total = total + acc[pl.ds(base + at, CHUNK), :]
            ref[pl.ds(at, CHUNK), :] = total.astype(ref.dtype)
            return 0

        lax.fori_loop(0, ref.shape[0] // CHUNK, step, 0)

    store(early_out, 0)
    store(late_out, early_rows)


def edge_sums(take_high, counts, packed, early, late):
    rows, width = early.shape[0] + late.shape[0], early.shape[1]
    smem = pl.BlockSpec(memory_space=pltpu.SMEM)
    vmem = pl.BlockSpec(memory_space=pltpu.VMEM)
    return pl.pallas_call(
        functools.partial(edge_kernel, take_high),
        out_shape=(
            jax.ShapeDtypeStruct(early.shape, jnp.bfloat16),
            jax.ShapeDtypeStruct(late.shape, jnp.bfloat16),
        ),
        in_specs=[smem, smem, vmem, vmem],
        out_specs=(vmem, vmem),
        scratch_shapes=[pltpu.VMEM((rows + 8, width), jnp.float32)] * (1 + ACCS),
        compiler_params=pltpu.CompilerParams(vmem_limit_bytes=40 * 1024 * 1024),
        cost_estimate=pl.CostEstimate(
            flops=16384 * width, bytes_accessed=4 * rows * width, transcendentals=0
        ),
        name="edge_sums",
    )(counts, packed, early, late)


def body(
    features,
    cotangent,
    edge_src,
    edge_dst,
    send_rows,
    recv_rows,
    in_degree,
    weight_self,
    weight_neigh,
):
    rows, width = features.shape
    half = width // 2
    early = rows - LATE
    dom_count = lax.axis_size("dom")
    chips = lax.axis_size("y")
    core = lax.axis_index("core")
    part_rows = rows * chips * 2
    contract_first = (((0,), (0,)), ((), ()))
    f32, bf16 = jnp.float32, jnp.bfloat16

    send_list = send_rows.reshape(-1)
    recv_list = recv_rows.reshape(-1)
    slot_count = send_list.shape[0]
    columns = lax.broadcasted_iota(jnp.int32, (slot_count, rows), 1)
    late_columns = lax.broadcasted_iota(jnp.int32, (slot_count, LATE), 1) + early
    pick_send = (send_list[:, None] == late_columns).astype(bf16)
    pick_recv = (recv_list[:, None] == columns).astype(bf16)
    is_mirror = lax.broadcasted_iota(jnp.int32, (rows, 1), 0) >= rows - MIRR
    late_mirror = is_mirror[early:]
    denominator = in_degree.reshape(-1).astype(f32)[:, None] + 1.0

    def over_dom(slots):
        return lax.all_to_all(slots, "dom", split_axis=0, concat_axis=0, tiled=True)

    def from_masters(values):
        slots = jnp.dot(pick_recv, values, preferred_element_type=f32).astype(bf16)
        return slots.reshape(dom_count, -1, values.shape[1])

    def at_mirrors(slots, values):
        arrived = lax.dot_general(
            pick_send, slots.reshape(slot_count, -1), contract_first, preferred_element_type=f32
        )
        return jnp.where(late_mirror, arrived.astype(bf16), values[early:])

    def mirrors_to_masters(late_values):
        slots = jnp.dot(pick_send, late_values, preferred_element_type=f32).astype(bf16)
        moved = over_dom(slots.reshape(dom_count, -1, width)).reshape(slot_count, width)
        return lax.dot_general(pick_recv, moved, contract_first, preferred_element_type=f32)

    def twin(values):
        return lax.ppermute(values, "core", [(0, 1), (1, 0)])

    def halves(values):
        mine = lax.dynamic_slice_in_dim(values, core * half, half, 1)
        other = lax.dynamic_slice_in_dim(values, (1 - core) * half, half, 1)
        return mine, other

    def chip_block(values):
        mine, other = halves(values)
        return jnp.concatenate([mine, twin(other)], axis=0)

    def gather(block):
        return lax.all_gather(block, "y", axis=0, tiled=True)

    def scatter(partial):
        return lax.psum_scatter(partial, "y", scatter_dimension=0, tiled=True)

    def whole_rows(block):
        count = block.shape[0] // 2
        mine = block[:count]
        other = twin(block[count:])
        return jnp.where(
            core == 0,
            jnp.concatenate([mine, other], axis=1),
            jnp.concatenate([other, mine], axis=1),
        )

    src, dst = edge_src.reshape(-1), edge_dst.reshape(-1)
    own_words = jnp.where(src >= 0, (dst << 16) | src, -1)
    words = jnp.stack([own_words, twin(own_words)])

    def table_row(row):
        member, within = (row // rows) ^ core, row % rows
        return jnp.where(
            within < early,
            member * early + within,
            (part_rows // rows) * early + member * LATE + within - early,
        )

    live = words >= 0
    counts = (jnp.sum(live.astype(jnp.int32), axis=1) + UNROLL - 1) // UNROLL
    packed = jnp.where(
        live,
        (table_row(words >> 16) << 16) | table_row(words & 0xFFFF),
        (part_rows << 16) | part_rows,
    )

    def edge_pass(take_high, early_table, late_table):
        return edge_sums(take_high, counts, packed, early_table, late_table)

    def partition_sums(early_part, late_part):
        late_block = scatter(late_part)
        late_block, early_part = lax.optimization_barrier((late_block, early_part))
        early_block = scatter(early_part)
        late_total = whole_rows(late_block)
        arrived = mirrors_to_masters(late_total)
        arrived, early_block = lax.optimization_barrier((arrived, early_block))
        totals = jnp.concatenate([whole_rows(early_block), late_total], axis=0).astype(f32)
        return totals + arrived

    early_block, sent = lax.optimization_barrier((chip_block(features[:early]), features))
    early_table = gather(early_block)
    late_rows = at_mirrors(over_dom(from_masters(sent)), features)
    early_table, late_rows = lax.optimization_barrier((early_table, late_rows))
    late_table = gather(chip_block(late_rows))
    early_part, late_part = edge_pass(False, early_table, late_table)
    totals = partition_sums(early_part, late_part)
    averaged = (totals / denominator).astype(bf16)

    pre = jnp.dot(features, weight_self, preferred_element_type=f32) + jnp.dot(
        averaged, weight_neigh, preferred_element_type=f32
    )
    gate_sig = jax.nn.sigmoid(pre)
    activated = (pre * gate_sig).astype(bf16)
    slope = gate_sig * (1.0 + pre * (1.0 - gate_sig))
    grad_pre = jnp.where(is_mirror, 0.0, cotangent.astype(f32) * slope).astype(bf16)
    grad_mean = (
        jnp.dot(grad_pre, weight_neigh.T, preferred_element_type=f32) / denominator
    ).astype(bf16)
    back_block, activated = lax.optimization_barrier((chip_block(grad_mean[:early]), activated))
    back_early = gather(back_block)
    local_self = lax.dot_general(features, grad_pre, contract_first, preferred_element_type=f32)
    local_neigh = lax.dot_general(averaged, grad_pre, contract_first, preferred_element_type=f32)
    self_term = jnp.dot(grad_pre, weight_self.T, preferred_element_type=f32)

    local_weights = jnp.concatenate([local_self, local_neigh], axis=1).astype(bf16)
    share = local_weights.reshape(dom_count, -1, 2 * width)
    slots = from_masters(jnp.concatenate([grad_mean, activated], axis=1))
    cap = slots.shape[1]
    moved = over_dom(jnp.concatenate([slots, share], axis=1))
    arrived = moved[:, :cap]
    late_rows = at_mirrors(arrived[:, :, :width], grad_mean)
    back_early, late_rows = lax.optimization_barrier((back_early, late_rows))
    back_late = gather(chip_block(late_rows))
    activated_late = at_mirrors(arrived[:, :, width:], activated)
    activated = jnp.concatenate([activated[:early], activated_late], axis=0)

    weight_sum = jnp.sum(moved[:, cap:].astype(f32), axis=0)
    back_late, weight_sum = lax.optimization_barrier((back_late, weight_sum))
    by_member = lax.all_gather(weight_sum, ("y", "core"), axis=0, tiled=False)

    early_part, late_part = edge_pass(True, back_early, back_late)
    weight_sum = jnp.sum(by_member, axis=0)
    weight_sums = over_dom(
        jnp.broadcast_to(weight_sum[None], (dom_count,) + weight_sum.shape)
    ).reshape(-1, 2 * width)
    back_sum = partition_sums(early_part, late_part)
    grad_features = jnp.where(is_mirror, 0.0, back_sum + self_term).astype(bf16)
    return activated, grad_features, weight_sums[:, :width], weight_sums[:, width:]


def solution(mesh):
    devices = mesh.devices
    split = Mesh(
        devices.reshape(devices.shape[0], devices.shape[1] // 2, 2), ("dom", "y", "core")
    )
    every = ("dom", "y", "core")
    member = ("y", "core")
    placed = (
        P(every, None),
        P(every, None),
        P("dom", member, None),
        P("dom", member, None),
        P("dom", member, None, None),
        P("dom", member, None, None),
        P("dom", member, None),
        P(),
        P(),
    )
    return jax.shard_map(
        body,
        mesh=split,
        in_specs=placed,
        out_specs=(P(every, None), P(every, None), P(), P()),
        check_vma=False,
    )
```

```python
import functools

import jax
import jax.numpy as jnp
from jax import lax
from jax.experimental import pallas as pl
from jax.experimental.pallas import tpu as pltpu
from jax.sharding import PartitionSpec as P

MIRR = 62
LATE = 64
UNROLL = 16
ACCS = 4
CHUNK = 128


def edge_kernel(
    take_high, counts_ref, packed_ref, early_ref, late_ref, early_out, late_out, table, *accs
):
    early_rows, late_rows = early_ref.shape[0], late_ref.shape[0]
    rows = early_rows + late_rows
    pad = table.shape[0] - rows

    def load(ref, base):
        def step(i, _):
            at = pl.multiple_of(i * CHUNK, CHUNK)
            table[pl.ds(base + at, CHUNK), :] = ref[pl.ds(at, CHUNK), :].astype(jnp.float32)
            for acc in accs:
                acc[pl.ds(base + at, CHUNK), :] = jnp.zeros((CHUNK, ref.shape[1]), jnp.float32)
            return 0

        lax.fori_loop(0, ref.shape[0] // CHUNK, step, 0)

    load(early_ref, 0)
    load(late_ref, early_rows)
    table[pl.ds(rows, pad), :] = jnp.zeros((pad, table.shape[1]), jnp.float32)

    one_row = (rows + pad, 1, table.shape[1])
    table_rows = table.reshape(one_row)
    acc_rows = [acc.reshape(one_row) for acc in accs]
    for which in range(2):

        def step(i, _):
            for group in range(UNROLL // ACCS):
                takes, places = [], []
                for k in range(ACCS):
                    word = packed_ref[which, i * UNROLL + group * ACCS + k]
                    low, high = word & 0xFFFF, word >> 16
                    takes.append(high if take_high else low)
                    places.append(low if take_high else high)
                sums = [acc_rows[k][places[k]] + table_rows[takes[k]] for k in range(ACCS)]
                for k in range(ACCS):
                    acc_rows[k][places[k]] = sums[k]
            return 0

        lax.fori_loop(0, counts_ref[which], step, 0)

    def store(ref, base):
        def step(i, _):
            at = pl.multiple_of(i * CHUNK, CHUNK)
            total = accs[0][pl.ds(base + at, CHUNK), :]
            for acc in accs[1:]:
                total = total + acc[pl.ds(base + at, CHUNK), :]
            ref[pl.ds(at, CHUNK), :] = total.astype(ref.dtype)
            return 0

        lax.fori_loop(0, ref.shape[0] // CHUNK, step, 0)

    store(early_out, 0)
    store(late_out, early_rows)


def edge_sums(take_high, counts, packed, early, late):
    rows, width = early.shape[0] + late.shape[0], early.shape[1]
    smem = pl.BlockSpec(memory_space=pltpu.SMEM)
    vmem = pl.BlockSpec(memory_space=pltpu.VMEM)
    return pl.pallas_call(
        functools.partial(edge_kernel, take_high),
        out_shape=(
            jax.ShapeDtypeStruct(early.shape, jnp.bfloat16),
            jax.ShapeDtypeStruct(late.shape, jnp.bfloat16),
        ),
        in_specs=[smem, smem, vmem, vmem],
        out_specs=(vmem, vmem),
        scratch_shapes=[pltpu.VMEM((rows + 8, width), jnp.float32)] * (1 + ACCS),
        compiler_params=pltpu.CompilerParams(vmem_limit_bytes=40 * 1024 * 1024),
        cost_estimate=pl.CostEstimate(
            flops=16384 * width, bytes_accessed=4 * rows * width, transcendentals=0
        ),
        name="edge_sums",
    )(counts, packed, early, late)


def body(
    features,
    cotangent,
    edge_src,
    edge_dst,
    send_rows,
    recv_rows,
    in_degree,
    weight_self,
    weight_neigh,
):
    rows, width = features.shape
    half = width // 2
    early = rows - LATE
    dom_count = lax.axis_size("dom")
    members = lax.axis_size("member")
    part_rows = rows * members
    contract_first = (((0,), (0,)), ((), ()))
    f32, bf16 = jnp.float32, jnp.bfloat16

    send_list = send_rows.reshape(-1)
    recv_list = recv_rows.reshape(-1)
    slot_count = send_list.shape[0]
    cap = slot_count // dom_count
    columns = lax.broadcasted_iota(jnp.int32, (slot_count, rows), 1)
    late_columns = lax.broadcasted_iota(jnp.int32, (slot_count, LATE), 1) + early
    pick_send = (send_list[:, None] == late_columns).astype(bf16)
    pick_recv = (recv_list[:, None] == columns).astype(bf16)
    is_mirror = lax.broadcasted_iota(jnp.int32, (rows, 1), 0) >= rows - MIRR
    late_mirror = is_mirror[early:]
    denominator = in_degree.reshape(-1).astype(f32)[:, None] + 1.0

    def over_dom(slots):
        return lax.all_to_all(slots, "dom", split_axis=0, concat_axis=0, tiled=True)

    def from_masters(values):
        slots = jnp.dot(pick_recv, values, preferred_element_type=f32).astype(bf16)
        return slots.reshape(dom_count, -1, values.shape[1])

    def at_mirrors(slots, values):
        arrived = lax.dot_general(
            pick_send, slots.reshape(slot_count, -1), contract_first, preferred_element_type=f32
        )
        return jnp.where(late_mirror, arrived.astype(bf16), values[early:])

    def over_member(blocks):
        return lax.all_to_all(blocks, "member", split_axis=0, concat_axis=0, tiled=True)

    def copies(values):
        halves = jnp.stack([values[:, :half], values[:, half:]])
        every = jnp.broadcast_to(halves[None], (members // 2,) + halves.shape)
        return every.reshape(members, -1, half)

    def gather(values):
        return over_member(copies(values)).reshape(-1, half)

    def member_sum(arrived):
        by_core = arrived.reshape((members // 2, 2) + arrived.shape[1:]).astype(f32)
        return jnp.concatenate([jnp.sum(by_core[:, core], axis=0) for core in (0, 1)], axis=1)

    src, dst = edge_src.reshape(-1), edge_dst.reshape(-1)

    def table_row(row):
        member, within = row // rows, row % rows
        return jnp.where(
            within < early, member * early + within, members * early + member * LATE + within - early
        )

    own_words = jnp.where(
        src >= 0, (table_row(dst) << 16) | table_row(src), (part_rows << 16) | part_rows
    )
    pairs = [(m, m ^ 1) for m in range(members)]
    packed = jnp.stack([own_words, lax.ppermute(own_words, "member", pairs)])
    live = packed < (part_rows << 16)
    counts = (jnp.sum(live.astype(jnp.int32), axis=1) + UNROLL - 1) // UNROLL

    def edge_pass(take_high, early_table, late_table):
        return edge_sums(take_high, counts, packed, early_table, late_table)

    def partition_sums(early_part, late_part, weight_sum=None):
        late_part = late_part.reshape(members, LATE, half)
        if weight_sum is not None:
            share = weight_sum.astype(bf16).reshape(-1, half)
            share = jnp.broadcast_to(share[None], (members,) + share.shape)
            late_part = jnp.concatenate([late_part, share], axis=1)
        late_arrived = over_member(late_part)
        late_arrived, early_part = lax.optimization_barrier((late_arrived, early_part))
        early_arrived = over_member(early_part.reshape(members, early, half))
        late_total = member_sum(late_arrived[:, :LATE])
        slots = jnp.dot(pick_send, late_total.astype(bf16), preferred_element_type=f32)
        slots = slots.astype(bf16).reshape(dom_count, -1, width)
        weight_sums = None
        if weight_sum is not None:
            share = jnp.sum(late_arrived[:, LATE:].astype(f32), axis=0).astype(bf16)
            share = share.reshape(-1, width)
            share = jnp.broadcast_to(share[None], (dom_count,) + share.shape)
            slots = jnp.concatenate([slots, share], axis=1)
        moved = over_dom(slots)
        if weight_sum is not None:
            weight_sums = moved[:, cap:].reshape(-1, 2 * width).astype(f32)
        arrived = lax.dot_general(
            pick_recv,
            moved[:, :cap].reshape(slot_count, width),
            contract_first,
            preferred_element_type=f32,
        )
        arrived, early_arrived = lax.optimization_barrier((arrived, early_arrived))
        totals = jnp.concatenate([member_sum(early_arrived), late_total], axis=0)
        return totals + arrived, weight_sums

    early_copies, sent = lax.optimization_barrier((copies(features[:early]), features))
    early_table = over_member(early_copies).reshape(-1, half)
    late_rows = at_mirrors(over_dom(from_masters(sent)), features)
    early_table, late_rows = lax.optimization_barrier((early_table, late_rows))
    late_table = gather(late_rows)
    early_part, late_part = edge_pass(False, early_table, late_table)
    totals, _ = partition_sums(early_part, late_part)
    averaged = (totals / denominator).astype(bf16)

    pre = jnp.dot(features, weight_self, preferred_element_type=f32) + jnp.dot(
        averaged, weight_neigh, preferred_element_type=f32
    )
    gate_sig = jax.nn.sigmoid(pre)
    activated = (pre * gate_sig).astype(bf16)
    slope = gate_sig * (1.0 + pre * (1.0 - gate_sig))
    grad_pre = jnp.where(is_mirror, 0.0, cotangent.astype(f32) * slope).astype(bf16)
    grad_mean = (
        jnp.dot(grad_pre, weight_neigh.T, preferred_element_type=f32) / denominator
    ).astype(bf16)
    early_copies, activated = lax.optimization_barrier((copies(grad_mean[:early]), activated))
    back_early = over_member(early_copies).reshape(-1, half)
    local_self = lax.dot_general(features, grad_pre, contract_first, preferred_element_type=f32)
    local_neigh = lax.dot_general(averaged, grad_pre, contract_first, preferred_element_type=f32)
    self_term = jnp.dot(grad_pre, weight_self.T, preferred_element_type=f32)

    local_weights = jnp.concatenate([local_self, local_neigh], axis=1).astype(bf16)
    share = local_weights.reshape(dom_count, -1, 2 * width)
    slots = from_masters(jnp.concatenate([grad_mean, activated], axis=1))
    moved = over_dom(jnp.concatenate([slots, share], axis=1))
    arrived = moved[:, :cap]
    late_rows = at_mirrors(arrived[:, :, :width], grad_mean)
    back_early, late_rows = lax.optimization_barrier((back_early, late_rows))
    back_late = gather(late_rows)
    activated_late = at_mirrors(arrived[:, :, width:], activated)
    activated = jnp.concatenate([activated[:early], activated_late], axis=0)

    weight_sum = jnp.sum(moved[:, cap:].astype(f32), axis=0)
    early_part, late_part = edge_pass(True, back_early, back_late)
    back_sum, weight_sums = partition_sums(early_part, late_part, weight_sum)
    grad_features = jnp.where(is_mirror, 0.0, back_sum + self_term).astype(bf16)
    return activated, grad_features, weight_sums[:, :width], weight_sums[:, width:]


def solution(mesh):
    placed = (
        P(("dom", "member"), None),
        P(("dom", "member"), None),
        P("dom", "member", None),
        P("dom", "member", None),
        P("dom", "member", None, None),
        P("dom", "member", None, None),
        P("dom", "member", None),
        P(),
        P(),
    )
    return jax.shard_map(
        body,
        mesh=mesh,
        in_specs=placed,
        out_specs=(P(("dom", "member"), None), P(("dom", "member"), None), P(), P()),
        check_vma=False,
    )
```

```python
import functools

import jax
import jax.numpy as jnp
from jax import lax
from jax.experimental import pallas as pl
from jax.experimental.pallas import tpu as pltpu
from jax.sharding import PartitionSpec as P

MIRR = 62
LATE = 64
UNROLL = 16
ACCS = 4
CHUNK = 128


def edge_kernel(take_high, bounds_ref, words_ref, table_ref, out_ref, words, table, *rest):
    accs, sems = rest[:-1], rest[-1]
    rows, width = table_ref.shape
    pad = table.shape[0] - rows
    lists = sems.shape[0]
    length = words.shape[0] // lists

    def copy(m):
        span = pl.ds(m * length, length)
        return pltpu.make_async_copy(words_ref.at[span], words.at[span], sems.at[m])

    for m in range(lists):

        @pl.when(bounds_ref[1, m] > bounds_ref[0, m])
        def _():
            copy(m).start()

    def load(i, _):
        span = pl.ds(pl.multiple_of(i * CHUNK, CHUNK), CHUNK)
        table[span, :] = table_ref[span, :].astype(jnp.float32)
        for acc in accs:
            acc[span, :] = jnp.zeros((CHUNK, width), jnp.float32)
        return 0

    lax.fori_loop(0, rows // CHUNK, load, 0)
    table[pl.ds(rows, pad), :] = jnp.zeros((pad, width), jnp.float32)

    one_row = (rows + pad, 1, width)
    table_rows = table.reshape(one_row)
    acc_rows = [acc.reshape(one_row) for acc in accs]
    for m in range(lists):

        def step(i, _):
            for group in range(UNROLL // ACCS):
                takes, places = [], []
                for k in range(ACCS):
                    word = words[m * length + i * UNROLL + group * ACCS + k]
                    low, high = word & 0xFFFF, word >> 16
                    takes.append(high if take_high else low)
                    places.append(low if take_high else high)
                sums = [acc_rows[k][places[k]] + table_rows[takes[k]] for k in range(ACCS)]
                for k in range(ACCS):
                    acc_rows[k][places[k]] = sums[k]
            return 0

        @pl.when(bounds_ref[1, m] > bounds_ref[0, m])
        def _():
            copy(m).wait()
            lax.fori_loop(bounds_ref[0, m], bounds_ref[1, m], step, 0)

    def store(i, _):
        span = pl.ds(pl.multiple_of(i * CHUNK, CHUNK), CHUNK)
        total = accs[0][span, :]
        for acc in accs[1:]:
            total = total + acc[span, :]
        out_ref[span, :] = total.astype(out_ref.dtype)
        return 0

    lax.fori_loop(0, rows // CHUNK, store, 0)


def edge_sums(take_high, bounds, words, table):
    rows, width = table.shape
    lists = bounds.shape[1]
    vmem = pl.BlockSpec(memory_space=pltpu.VMEM)
    return pl.pallas_call(
        functools.partial(edge_kernel, take_high),
        out_shape=jax.ShapeDtypeStruct((rows, width), jnp.bfloat16),
        in_specs=[
            pl.BlockSpec(memory_space=pltpu.SMEM),
            pl.BlockSpec(memory_space=pl.ANY),
            vmem,
        ],
        out_specs=vmem,
        scratch_shapes=[pltpu.SMEM(words.shape, jnp.int32)]
        + [pltpu.VMEM((rows + 8, width), jnp.float32)] * (1 + ACCS)
        + [pltpu.SemaphoreType.DMA((lists,))],
        compiler_params=pltpu.CompilerParams(vmem_limit_bytes=40 * 1024 * 1024),
        cost_estimate=pl.CostEstimate(
            flops=16384 * width, bytes_accessed=4 * rows * width, transcendentals=0
        ),
        name="edge_sums",
    )(bounds, words, table)


def body(
    features,
    cotangent,
    edge_src,
    edge_dst,
    send_rows,
    recv_rows,
    in_degree,
    weight_self,
    weight_neigh,
):
    rows, width = features.shape
    half = width // 2
    early = rows - LATE
    dom_count = lax.axis_size("dom")
    members = lax.axis_size("member")
    part_rows = rows * members
    contract_first = (((0,), (0,)), ((), ()))
    f32, bf16 = jnp.float32, jnp.bfloat16

    send_list = send_rows.reshape(-1)
    recv_list = recv_rows.reshape(-1)
    slot_count = send_list.shape[0]
    cap = slot_count // dom_count
    columns = lax.broadcasted_iota(jnp.int32, (slot_count, rows), 1)
    late_columns = lax.broadcasted_iota(jnp.int32, (slot_count, LATE), 1) + early
    pick_send = (send_list[:, None] == late_columns).astype(bf16)
    pick_recv = (recv_list[:, None] == columns).astype(bf16)
    is_mirror = lax.broadcasted_iota(jnp.int32, (rows, 1), 0) >= rows - MIRR
    late_mirror = is_mirror[early:]
    denominator = in_degree.reshape(-1).astype(f32)[:, None] + 1.0

    def over_dom(slots):
        return lax.all_to_all(slots, "dom", split_axis=0, concat_axis=0, tiled=True)

    def from_masters(values):
        slots = jnp.dot(pick_recv, values, preferred_element_type=f32).astype(bf16)
        return slots.reshape(dom_count, -1, values.shape[1])

    def at_mirrors(slots, values):
        arrived = lax.dot_general(
            pick_send, slots.reshape(slot_count, -1), contract_first, preferred_element_type=f32
        )
        return jnp.where(late_mirror, arrived.astype(bf16), values[early:])

    def over_member(blocks):
        return lax.all_to_all(blocks, "member", split_axis=0, concat_axis=0, tiled=True)

    def gather(values):
        halves = jnp.stack([values[:, :half], values[:, half:]])
        every = jnp.broadcast_to(halves[None], (members // 2,) + halves.shape)
        return over_member(every.reshape(members, rows, half)).reshape(-1, half)

    def member_sum(arrived):
        by_core = arrived.reshape((members // 2, 2) + arrived.shape[1:]).astype(f32)
        return jnp.concatenate([jnp.sum(by_core[:, core], axis=0) for core in (0, 1)], axis=1)

    src, dst = edge_src.reshape(-1), edge_dst.reshape(-1)
    words = jnp.where(src >= 0, (dst << 16) | src, (part_rows << 16) | part_rows)
    mine = words.reshape(1, -1)
    index = lax.axis_index("member")
    bit = 1
    while bit < members:
        theirs = lax.ppermute(mine, "member", [(m, m ^ bit) for m in range(members)])
        low = (index & bit) == 0
        mine = jnp.concatenate([jnp.where(low, mine, theirs), jnp.where(low, theirs, mine)])
        bit *= 2
    blocks = jnp.sum((mine < (part_rows << 16)).astype(jnp.int32), axis=1)
    blocks = (blocks + UNROLL - 1) // UNROLL
    before = jnp.sum(
        jnp.where(
            lax.broadcasted_iota(jnp.int32, (members, members), 1)
            < lax.broadcasted_iota(jnp.int32, (members, members), 0),
            blocks[None, :],
            0,
        ),
        axis=1,
    )
    total = jnp.sum(blocks)
    chips = members // 2
    chip = index >> 1
    bounds = jnp.stack(
        [jnp.clip(lax.div(total * at, chips) - before, 0, blocks) for at in (chip, chip + 1)]
    )
    words = mine.reshape(-1)

    def partition_sums(table, take_high, weight_sum=None):
        part = edge_sums(take_high, bounds, words, table).reshape(members, rows, half)
        if weight_sum is not None:
            share = weight_sum.astype(bf16).reshape(-1, half)
            share = jnp.broadcast_to(share[None], (members,) + share.shape)
            part = jnp.concatenate([part, share], axis=1)
        arrived = over_member(part)
        totals = member_sum(arrived[:, :rows])
        slots = jnp.dot(pick_send, totals[early:].astype(bf16), preferred_element_type=f32)
        slots = slots.astype(bf16).reshape(dom_count, -1, width)
        weight_sums = None
        if weight_sum is not None:
            share = jnp.sum(arrived[:, rows:].astype(f32), axis=0).astype(bf16)
            share = share.reshape(-1, width)
            share = jnp.broadcast_to(share[None], (dom_count,) + share.shape)
            slots = jnp.concatenate([slots, share], axis=1)
        moved = over_dom(slots)
        if weight_sum is not None:
            weight_sums = moved[:, cap:].reshape(-1, 2 * width).astype(f32)
        from_mirrors = lax.dot_general(
            pick_recv,
            moved[:, :cap].reshape(slot_count, width),
            contract_first,
            preferred_element_type=f32,
        )
        return totals + from_mirrors, weight_sums

    late_rows = at_mirrors(over_dom(from_masters(features)), features)
    table = gather(jnp.concatenate([features[:early], late_rows], axis=0))
    totals, _ = partition_sums(table, False)
    averaged = (totals / denominator).astype(bf16)

    pre = jnp.dot(features, weight_self, preferred_element_type=f32) + jnp.dot(
        averaged, weight_neigh, preferred_element_type=f32
    )
    gate_sig = jax.nn.sigmoid(pre)
    activated = (pre * gate_sig).astype(bf16)
    slope = gate_sig * (1.0 + pre * (1.0 - gate_sig))
    grad_pre = jnp.where(is_mirror, 0.0, cotangent.astype(f32) * slope).astype(bf16)
    grad_mean = (
        jnp.dot(grad_pre, weight_neigh.T, preferred_element_type=f32) / denominator
    ).astype(bf16)
    local_self = lax.dot_general(features, grad_pre, contract_first, preferred_element_type=f32)
    local_neigh = lax.dot_general(averaged, grad_pre, contract_first, preferred_element_type=f32)
    self_term = jnp.dot(grad_pre, weight_self.T, preferred_element_type=f32)

    local_weights = jnp.concatenate([local_self, local_neigh], axis=1).astype(bf16)
    share = local_weights.reshape(dom_count, -1, 2 * width)
    slots = from_masters(jnp.concatenate([grad_mean, activated], axis=1))
    moved = over_dom(jnp.concatenate([slots, share], axis=1))
    arrived = moved[:, :cap]
    late_rows = at_mirrors(arrived[:, :, :width], grad_mean)
    table = gather(jnp.concatenate([grad_mean[:early], late_rows], axis=0))
    activated_late = at_mirrors(arrived[:, :, width:], activated)
    activated = jnp.concatenate([activated[:early], activated_late], axis=0)

    weight_sum = jnp.sum(moved[:, cap:].astype(f32), axis=0)
    back_sum, weight_sums = partition_sums(table, True, weight_sum)
    grad_features = jnp.where(is_mirror, 0.0, back_sum + self_term).astype(bf16)
    return activated, grad_features, weight_sums[:, :width], weight_sums[:, width:]


def solution(mesh):
    placed = (
        P(("dom", "member"), None),
        P(("dom", "member"), None),
        P("dom", "member", None),
        P("dom", "member", None),
        P("dom", "member", None, None),
        P("dom", "member", None, None),
        P("dom", "member", None),
        P(),
        P(),
    )
    return jax.shard_map(
        body,
        mesh=mesh,
        in_specs=placed,
        out_specs=(P(("dom", "member"), None), P(("dom", "member"), None), P(), P()),
        check_vma=False,
    )
```

```python
import functools

import jax
import jax.numpy as jnp
from jax import lax
from jax.experimental import pallas as pl
from jax.experimental.pallas import tpu as pltpu
from jax.sharding import Mesh, PartitionSpec as P

MIRR = 62
LATE = 64
FIRST = 128
UNROLL = 16
ACCS = 4
CHUNK = 64


def edge_kernel(
    take_high,
    bounds_ref,
    words_ref,
    early_ref,
    late_ref,
    first_out,
    last_out,
    words,
    table,
    *rest,
):
    accs, sems = rest[:-1], rest[-1]
    lists = sems.shape[0]
    width = late_ref.shape[1]
    early, late = early_ref.shape[0] // lists, late_ref.shape[0] // lists
    first = first_out.shape[0] // lists
    last = early + late - first
    rows = lists * (early + late)
    pad = table.shape[0] - rows
    column = pl.multiple_of(bounds_ref[2, 0] * width, width)
    length = words.shape[0] // lists

    def copy(m):
        span = pl.ds(m * length, length)
        return pltpu.make_async_copy(words_ref.at[span], words.at[span], sems.at[m])

    for m in range(lists):

        @pl.when(bounds_ref[1, m] > bounds_ref[0, m])
        def _():
            copy(m).start()

    def load(m, _):
        def put(target, count, source):
            for at in range(0, count, CHUNK):
                span = pl.ds(pl.multiple_of(target + at, CHUNK), CHUNK)
                table[span, :] = source(at).astype(jnp.float32)
                for acc in accs:
                    acc[span, :] = jnp.zeros((CHUNK, width), jnp.float32)

        def from_early(at):
            return early_ref[
                pl.ds(pl.multiple_of(m * early + at, CHUNK), CHUNK), pl.ds(column, width)
            ]

        def from_late(at):
            return late_ref[pl.ds(pl.multiple_of(m * late + at, CHUNK), CHUNK), :]

        put(m * first, first, from_early)
        put(lists * first + m * last, early - first, lambda at: from_early(first + at))
        put(lists * first + m * last + early - first, late, from_late)
        return 0

    lax.fori_loop(0, lists, load, 0)
    table[pl.ds(rows, pad), :] = jnp.zeros((pad, width), jnp.float32)

    one_row = (rows + pad, 1, width)
    table_rows = table.reshape(one_row)
    acc_rows = [acc.reshape(one_row) for acc in accs]
    for m in range(lists):

        def step(i, _):
            for group in range(UNROLL // ACCS):
                takes, places = [], []
                for k in range(ACCS):
                    word = words[m * length + i * UNROLL + group * ACCS + k]
                    low, high = word & 0xFFFF, word >> 16
                    takes.append(high if take_high else low)
                    places.append(low if take_high else high)
                sums = [acc_rows[k][places[k]] + table_rows[takes[k]] for k in range(ACCS)]
                for k in range(ACCS):
                    acc_rows[k][places[k]] = sums[k]
            return 0

        @pl.when(bounds_ref[1, m] > bounds_ref[0, m])
        def _():
            copy(m).wait()
            lax.fori_loop(bounds_ref[0, m], bounds_ref[1, m], step, 0)

    def store(ref, base):
        def step(i, _):
            at = pl.multiple_of(i * CHUNK, CHUNK)
            total = accs[0][pl.ds(base + at, CHUNK), :]
            for acc in accs[1:]:
                total = total + acc[pl.ds(base + at, CHUNK), :]
            ref[pl.ds(at, CHUNK), :] = total.astype(ref.dtype)
            return 0

        lax.fori_loop(0, ref.shape[0] // CHUNK, step, 0)

    store(first_out, 0)
    store(last_out, first_out.shape[0])


def edge_sums(take_high, bounds, words, early, late):
    lists, width = bounds.shape[1], late.shape[1]
    rows = early.shape[0] + late.shape[0]
    smem = pl.BlockSpec(memory_space=pltpu.SMEM)
    vmem = pl.BlockSpec(memory_space=pltpu.VMEM)
    return pl.pallas_call(
        functools.partial(edge_kernel, take_high),
        out_shape=(
            jax.ShapeDtypeStruct((lists * FIRST, width), jnp.bfloat16),
            jax.ShapeDtypeStruct((rows - lists * FIRST, width), jnp.bfloat16),
        ),
        in_specs=[smem, pl.BlockSpec(memory_space=pl.ANY), vmem, vmem],
        out_specs=(vmem, vmem),
        scratch_shapes=[pltpu.SMEM(words.shape, jnp.int32)]
        + [pltpu.VMEM((rows + 8, width), jnp.float32)] * (1 + ACCS)
        + [pltpu.SemaphoreType.DMA((lists,))],
        compiler_params=pltpu.CompilerParams(vmem_limit_bytes=40 * 1024 * 1024),
        cost_estimate=pl.CostEstimate(
            flops=16384 * width, bytes_accessed=4 * rows * width, transcendentals=0
        ),
        name="edge_sums",
    )(bounds, words, early, late)


def body(
    features,
    cotangent,
    edge_src,
    edge_dst,
    send_rows,
    recv_rows,
    in_degree,
    weight_self,
    weight_neigh,
):
    rows, width = features.shape
    half = width // 2
    early = rows - LATE
    dom_count = lax.axis_size("dom")
    member = ("y", "core")
    chips = lax.axis_size("y")
    members = 2 * chips
    core = lax.axis_index("core")
    part_rows = rows * members
    contract_first = (((0,), (0,)), ((), ()))
    f32, bf16 = jnp.float32, jnp.bfloat16

    send_list = send_rows.reshape(-1)
    recv_list = recv_rows.reshape(-1)
    slot_count = send_list.shape[0]
    cap = slot_count // dom_count
    columns = lax.broadcasted_iota(jnp.int32, (slot_count, rows), 1)
    late_columns = lax.broadcasted_iota(jnp.int32, (slot_count, LATE), 1) + early
    pick_send = (send_list[:, None] == late_columns).astype(bf16)
    pick_recv = (recv_list[:, None] == columns).astype(bf16)
    is_mirror = lax.broadcasted_iota(jnp.int32, (rows, 1), 0) >= rows - MIRR
    late_mirror = is_mirror[early:]
    denominator = in_degree.reshape(-1).astype(f32)[:, None] + 1.0

    def over_dom(slots):
        return lax.all_to_all(slots, "dom", split_axis=0, concat_axis=0, tiled=True)

    def from_masters(values):
        slots = jnp.dot(pick_recv, values, preferred_element_type=f32).astype(bf16)
        return slots.reshape(dom_count, -1, values.shape[1])

    def at_mirrors(slots, values):
        arrived = lax.dot_general(
            pick_send, slots.reshape(slot_count, -1), contract_first, preferred_element_type=f32
        )
        return jnp.where(late_mirror, arrived.astype(bf16), values[early:])

    def over_member(blocks):
        return lax.all_to_all(blocks, member, split_axis=0, concat_axis=0, tiled=True)

    def gather(values):
        halves = jnp.stack([values[:, :half], values[:, half:]])
        every = jnp.broadcast_to(halves[None], (members // 2,) + halves.shape)
        return over_member(every.reshape(members, -1, half)).reshape(-1, half)

    def twin(values):
        return lax.ppermute(values, "core", [(0, 1), (1, 0)])

    def whole_rows(block):
        count = block.shape[0] // 2
        mine = lax.dynamic_slice_in_dim(block, core * count, count, 0)
        other = twin(lax.dynamic_slice_in_dim(block, (1 - core) * count, count, 0))
        return jnp.where(
            core == 0,
            jnp.concatenate([mine, other], axis=1),
            jnp.concatenate([other, mine], axis=1),
        )

    def member_sum(arrived):
        by_core = arrived.reshape((members // 2, 2) + arrived.shape[1:]).astype(f32)
        return jnp.concatenate([jnp.sum(by_core[:, core], axis=0) for core in (0, 1)], axis=1)

    src, dst = edge_src.reshape(-1), edge_dst.reshape(-1)
    def table_row(row):
        at, within = row // rows, row % rows
        return jnp.where(
            within < FIRST,
            at * FIRST + within,
            members * FIRST + at * (rows - FIRST) + within - FIRST,
        )

    words = jnp.where(
        src >= 0, (table_row(dst) << 16) | table_row(src), (part_rows << 16) | part_rows
    )
    chip = lax.axis_index("y")

    def both(mine, theirs, low):
        return jnp.concatenate([jnp.where(low, mine, theirs), jnp.where(low, theirs, mine)])

    mine = words.reshape(1, -1)
    mine = both(mine, twin(mine), core == 0)
    bit = 1
    while bit < chips:
        theirs = lax.ppermute(mine, "y", [(y, y ^ bit) for y in range(chips)])
        mine = both(mine, theirs, (chip & bit) == 0)
        bit *= 2
    blocks = jnp.sum((mine < (part_rows << 16)).astype(jnp.int32), axis=1)
    blocks = (blocks + UNROLL - 1) // UNROLL
    before = jnp.sum(
        jnp.where(
            lax.broadcasted_iota(jnp.int32, (members, members), 1)
            < lax.broadcasted_iota(jnp.int32, (members, members), 0),
            blocks[None, :],
            0,
        ),
        axis=1,
    )
    total = jnp.sum(blocks)
    bounds = jnp.stack(
        [jnp.clip(lax.div(total * at, chips) - before, 0, blocks) for at in (chip, chip + 1)]
        + [jnp.broadcast_to(core, blocks.shape)]
    )
    words = mine.reshape(-1)

    def partition_sums(early_table, late_table, take_high, weight_sum=None):
        first, part = edge_sums(take_high, bounds, words, early_table, late_table)
        first_block = lax.psum_scatter(first, "y", scatter_dimension=0, tiled=True)
        part = part.reshape(members, -1, half)
        last = part.shape[1]
        if weight_sum is not None:
            share = weight_sum.astype(bf16).reshape(-1, half)
            share = jnp.broadcast_to(share[None], (members,) + share.shape)
            part = jnp.concatenate([part, share], axis=1)
        arrived = over_member(part)
        last_total = member_sum(arrived[:, :last])
        slots = jnp.dot(pick_send, last_total[-LATE:].astype(bf16), preferred_element_type=f32)
        slots = slots.astype(bf16).reshape(dom_count, -1, width)
        weight_sums = None
        if weight_sum is not None:
            share = jnp.sum(arrived[:, last:].astype(f32), axis=0).astype(bf16)
            share = share.reshape(-1, width)
            share = jnp.broadcast_to(share[None], (dom_count,) + share.shape)
            slots = jnp.concatenate([slots, share], axis=1)
        moved = over_dom(slots)
        if weight_sum is not None:
            weight_sums = moved[:, cap:].reshape(-1, 2 * width).astype(f32)
        from_mirrors = lax.dot_general(
            pick_recv,
            moved[:, :cap].reshape(slot_count, width),
            contract_first,
            preferred_element_type=f32,
        )
        from_mirrors, first_block = lax.optimization_barrier((from_mirrors, first_block))
        totals = jnp.concatenate([whole_rows(first_block), last_total], axis=0)
        return totals + from_mirrors, weight_sums

    early_table = lax.all_gather(features[:early], member, axis=0, tiled=True)
    late_rows = at_mirrors(over_dom(from_masters(features)), features)
    totals, _ = partition_sums(early_table, gather(late_rows), False)
    averaged = (totals / denominator).astype(bf16)

    pre = jnp.dot(features, weight_self, preferred_element_type=f32) + jnp.dot(
        averaged, weight_neigh, preferred_element_type=f32
    )
    gate_sig = jax.nn.sigmoid(pre)
    activated = (pre * gate_sig).astype(bf16)
    slope = gate_sig * (1.0 + pre * (1.0 - gate_sig))
    grad_pre = jnp.where(is_mirror, 0.0, cotangent.astype(f32) * slope).astype(bf16)
    grad_mean = (
        jnp.dot(grad_pre, weight_neigh.T, preferred_element_type=f32) / denominator
    ).astype(bf16)
    early_table = lax.all_gather(grad_mean[:early], member, axis=0, tiled=True)
    local_self = lax.dot_general(features, grad_pre, contract_first, preferred_element_type=f32)
    local_neigh = lax.dot_general(averaged, grad_pre, contract_first, preferred_element_type=f32)
    self_term = jnp.dot(grad_pre, weight_self.T, preferred_element_type=f32)

    local_weights = jnp.concatenate([local_self, local_neigh], axis=1).astype(bf16)
    share = local_weights.reshape(dom_count, -1, 2 * width)
    slots = from_masters(jnp.concatenate([grad_mean, activated], axis=1))
    moved = over_dom(jnp.concatenate([slots, share], axis=1))
    arrived = moved[:, :cap]
    late_rows = at_mirrors(arrived[:, :, :width], grad_mean)
    late_table = gather(late_rows)
    activated_late = at_mirrors(arrived[:, :, width:], activated)
    activated = jnp.concatenate([activated[:early], activated_late], axis=0)

    weight_sum = jnp.sum(moved[:, cap:].astype(f32), axis=0)
    back_sum, weight_sums = partition_sums(early_table, late_table, True, weight_sum)
    grad_features = jnp.where(is_mirror, 0.0, back_sum + self_term).astype(bf16)
    return activated, grad_features, weight_sums[:, :width], weight_sums[:, width:]


def solution(mesh):
    devices = mesh.devices
    split = Mesh(
        devices.reshape(devices.shape[0], devices.shape[1] // 2, 2), ("dom", "y", "core")
    )
    every = ("dom", "y", "core")
    member = ("y", "core")
    placed = (
        P(every, None),
        P(every, None),
        P("dom", member, None),
        P("dom", member, None),
        P("dom", member, None, None),
        P("dom", member, None, None),
        P("dom", member, None),
        P(),
        P(),
    )
    return jax.shard_map(
        body,
        mesh=split,
        in_specs=placed,
        out_specs=(P(every, None), P(every, None), P(), P()),
        check_vma=False,
    )
```

```python
import jax
import jax.numpy as jnp
from jax import lax
from jax.experimental import pallas as pl
from jax.experimental.pallas import tpu as pltpu
from jax.sharding import Mesh, PartitionSpec as P

MIRR = 62
LATE = 64
UNROLL = 16
ACCS = 8
CHUNK = 128
WINDOW = 1024


def edge_kernel(bounds_ref, words_ref, table_ref, out_ref, words, table, *rest):
    accs, sems = rest[:-1], rest[-1]
    rows, width = table_ref.shape
    own = out_ref.shape[0]
    lists = sems.shape[0]
    length = words.shape[0] // lists

    def windows(m, act):
        def step(at, _):
            span = pl.ds(pl.multiple_of(m * length + at * WINDOW, WINDOW), WINDOW)
            act(pltpu.make_async_copy(words_ref.at[span], words.at[span], sems.at[m]))
            return 0

        last = (bounds_ref[1, m] + (WINDOW - 1)) // WINDOW
        lax.fori_loop(bounds_ref[0, m] // WINDOW, last, step, 0)

    for m in range(lists):
        windows(m, lambda copy: copy.start())

    def load(i, _):
        span = pl.ds(pl.multiple_of(i * CHUNK, CHUNK), CHUNK)
        table[span, :] = table_ref[span, :].astype(jnp.float32)
        return 0

    lax.fori_loop(0, rows // CHUNK, load, 0)

    def clear(i, _):
        span = pl.ds(pl.multiple_of(i * CHUNK, CHUNK), CHUNK)
        for acc in accs:
            acc[span, :] = jnp.zeros((CHUNK, width), jnp.float32)
        return 0

    lax.fori_loop(0, own // CHUNK, clear, 0)

    table_rows = table.reshape((rows, 1, width))
    acc_rows = [acc.reshape((own, 1, width)) for acc in accs]

    def add(base, count):
        takes, places = [], []
        for k in range(count):
            word = words[base + k]
            takes.append(word & 0xFFFF)
            places.append((word >> 16) & (own - 1))
        sums = [acc_rows[k][places[k]] + table_rows[takes[k]] for k in range(count)]
        for k in range(count):
            acc_rows[k][places[k]] = sums[k]

    for m in range(lists):
        windows(m, lambda copy: copy.wait())
        low, high = bounds_ref[0, m], bounds_ref[1, m]
        blocks = (high - low) // UNROLL

        def block(i, _):
            for group in range(UNROLL // ACCS):
                add(m * length + low + i * UNROLL + group * ACCS, ACCS)
            return 0

        def single(i, _):
            add(m * length + i, 1)
            return 0

        lax.fori_loop(0, blocks, block, 0)
        lax.fori_loop(low + blocks * UNROLL, high, single, 0)

    def store(i, _):
        span = pl.ds(pl.multiple_of(i * CHUNK, CHUNK), CHUNK)
        total = accs[0][span, :]
        for acc in accs[1:]:
            total = total + acc[span, :]
        out_ref[span, :] = total
        return 0

    lax.fori_loop(0, own // CHUNK, store, 0)


def edge_sums(bounds, words, table):
    rows, width = table.shape
    lists = bounds.shape[1]
    own = 2 * (rows // lists)
    vmem = pl.BlockSpec(memory_space=pltpu.VMEM)
    return pl.pallas_call(
        edge_kernel,
        out_shape=jax.ShapeDtypeStruct((own, width), jnp.float32),
        in_specs=[
            pl.BlockSpec(memory_space=pltpu.SMEM),
            pl.BlockSpec(memory_space=pl.ANY),
            vmem,
        ],
        out_specs=vmem,
        scratch_shapes=[
            pltpu.SMEM(words.shape, jnp.int32),
            pltpu.VMEM((rows, width), jnp.float32),
        ]
        + [pltpu.VMEM((own, width), jnp.float32)] * ACCS
        + [pltpu.SemaphoreType.DMA((lists,))],
        compiler_params=pltpu.CompilerParams(vmem_limit_bytes=40 * 1024 * 1024),
        cost_estimate=pl.CostEstimate(
            flops=16384 * width, bytes_accessed=4 * rows * width, transcendentals=0
        ),
        name="edge_sums",
    )(bounds, words, table)


def body(
    features,
    cotangent,
    edge_src,
    edge_dst,
    send_rows,
    recv_rows,
    in_degree,
    weight_self,
    weight_neigh,
):
    rows, width = features.shape
    half = width // 2
    early = rows - LATE
    dom_count = lax.axis_size("dom")
    member = ("y", "core")
    chips = lax.axis_size("y")
    members = 2 * chips
    core = lax.axis_index("core")
    chip = lax.axis_index("y")
    part_rows = rows * members
    contract_first = (((0,), (0,)), ((), ()))
    f32, bf16 = jnp.float32, jnp.bfloat16

    send_list = send_rows.reshape(-1)
    recv_list = recv_rows.reshape(-1)
    slot_count = send_list.shape[0]
    cap = slot_count // dom_count
    columns = lax.broadcasted_iota(jnp.int32, (slot_count, rows), 1)
    late_columns = lax.broadcasted_iota(jnp.int32, (slot_count, LATE), 1) + early
    pick_send = (send_list[:, None] == late_columns).astype(bf16)
    pick_recv = (recv_list[:, None] == columns).astype(bf16)
    is_mirror = lax.broadcasted_iota(jnp.int32, (rows, 1), 0) >= rows - MIRR
    late_mirror = is_mirror[early:]
    denominator = in_degree.reshape(-1).astype(f32)[:, None] + 1.0

    def over_dom(slots):
        return lax.all_to_all(slots, "dom", split_axis=0, concat_axis=0, tiled=True)

    def from_masters(values):
        slots = jnp.dot(pick_recv, values, preferred_element_type=f32).astype(bf16)
        return slots.reshape(dom_count, -1, values.shape[1])

    def at_mirrors(slots, values):
        arrived = lax.dot_general(
            pick_send, slots.reshape(slot_count, -1), contract_first, preferred_element_type=f32
        )
        return jnp.where(late_mirror, arrived.astype(bf16), values[early:])

    def over_member(blocks):
        return lax.all_to_all(blocks, member, split_axis=0, concat_axis=0, tiled=True)

    def gather(values):
        halves = jnp.stack([values[:, :half], values[:, half:]])
        every = jnp.broadcast_to(halves[None], (members // 2,) + halves.shape)
        return over_member(every.reshape(members, rows, half)).reshape(-1, half)

    def twin(values):
        return lax.ppermute(values, "core", [(0, 1), (1, 0)])

    def spread(values, combine):
        values = combine(values, twin(values), core == 0)
        bit = 1
        while bit < chips:
            theirs = lax.ppermute(values, "y", [(y, y ^ bit) for y in range(chips)])
            values = combine(values, theirs, (chip & bit) == 0)
            bit *= 2
        return values

    def edge_lists(place, take):
        words = jnp.where(place >= 0, (place << 16) | take, part_rows << 16)
        words = lax.sort(words.reshape(1, -1), dimension=1)
        words = spread(
            words,
            lambda mine, theirs, low: jnp.concatenate(
                [jnp.where(low, mine, theirs), jnp.where(low, theirs, mine)]
            ),
        )
        bounds = jnp.stack(
            [
                jnp.sum((words < (at * (2 * rows) << 16)).astype(jnp.int32), axis=1)
                for at in (chip, chip + 1)
            ]
        )
        return bounds, words.reshape(-1)

    def row_sums(lists, table):
        block = edge_sums(*lists, table)
        mine = lax.dynamic_slice_in_dim(block, core * rows, rows, 0)
        other = lax.dynamic_slice_in_dim(block, (1 - core) * rows, rows, 0)
        other = twin(other.astype(bf16)).astype(f32)
        return jnp.where(
            core == 0,
            jnp.concatenate([mine, other], axis=1),
            jnp.concatenate([other, mine], axis=1),
        )

    def mirror_slots(totals):
        slots = jnp.dot(pick_send, totals[early:].astype(bf16), preferred_element_type=f32)
        return slots.astype(bf16).reshape(dom_count, -1, width)

    def add_at_masters(slots):
        return lax.dot_general(
            pick_recv, slots.reshape(slot_count, width), contract_first, preferred_element_type=f32
        )

    src, dst = edge_src.reshape(-1), edge_dst.reshape(-1)
    slots, src, dst = lax.optimization_barrier((from_masters(features), src, dst))
    lists = edge_lists(dst, src)
    late_rows = at_mirrors(over_dom(slots), features)
    table = gather(jnp.concatenate([features[:early], late_rows], axis=0))
    totals = row_sums(lists, table)
    totals, src, dst = lax.optimization_barrier((totals, src, dst))
    lists = edge_lists(src, dst)
    totals = totals + add_at_masters(over_dom(mirror_slots(totals)))
    averaged = (totals / denominator).astype(bf16)

    pre = jnp.dot(features, weight_self, preferred_element_type=f32) + jnp.dot(
        averaged, weight_neigh, preferred_element_type=f32
    )
    gate_sig = jax.nn.sigmoid(pre)
    activated = (pre * gate_sig).astype(bf16)
    slope = gate_sig * (1.0 + pre * (1.0 - gate_sig))
    grad_pre = jnp.where(is_mirror, 0.0, cotangent.astype(f32) * slope).astype(bf16)
    grad_mean = (
        jnp.dot(grad_pre, weight_neigh.T, preferred_element_type=f32) / denominator
    ).astype(bf16)
    local_self = lax.dot_general(features, grad_pre, contract_first, preferred_element_type=f32)
    local_neigh = lax.dot_general(averaged, grad_pre, contract_first, preferred_element_type=f32)
    self_term = jnp.dot(grad_pre, weight_self.T, preferred_element_type=f32)

    local_weights = jnp.concatenate([local_self, local_neigh], axis=1).astype(bf16)
    share = local_weights.reshape(dom_count, -1, 2 * width)
    slots = from_masters(jnp.concatenate([grad_mean, activated], axis=1))
    moved = over_dom(jnp.concatenate([slots, share], axis=1))
    arrived = moved[:, :cap]
    late_rows = at_mirrors(arrived[:, :, :width], grad_mean)
    table = gather(jnp.concatenate([grad_mean[:early], late_rows], axis=0))
    activated_late = at_mirrors(arrived[:, :, width:], activated)
    activated = jnp.concatenate([activated[:early], activated_late], axis=0)

    weight_sum = spread(
        jnp.sum(moved[:, cap:].astype(f32), axis=0), lambda mine, theirs, low: mine + theirs
    )
    share = weight_sum.astype(bf16).reshape(-1, width)
    share = jnp.broadcast_to(share[None], (dom_count,) + share.shape)
    totals = row_sums(lists, table)
    moved = over_dom(jnp.concatenate([mirror_slots(totals), share], axis=1))
    weight_sums = moved[:, cap:].reshape(-1, 2 * width).astype(f32)
    back_sum = totals + add_at_masters(moved[:, :cap])
    grad_features = jnp.where(is_mirror, 0.0, back_sum + self_term).astype(bf16)
    return activated, grad_features, weight_sums[:, :width], weight_sums[:, width:]


def solution(mesh):
    devices = mesh.devices
    split = Mesh(
        devices.reshape(devices.shape[0], devices.shape[1] // 2, 2), ("dom", "y", "core")
    )
    every = ("dom", "y", "core")
    member = ("y", "core")
    placed = (
        P(every, None),
        P(every, None),
        P("dom", member, None),
        P("dom", member, None),
        P("dom", member, None, None),
        P("dom", member, None, None),
        P("dom", member, None),
        P(),
        P(),
    )
    return jax.shard_map(
        body,
        mesh=split,
        in_specs=placed,
        out_specs=(P(every, None), P(every, None), P(), P()),
        check_vma=False,
    )
```

```python
import jax
import jax.numpy as jnp
from jax import lax
from jax.experimental import pallas as pl
from jax.experimental.pallas import tpu as pltpu
from jax.sharding import Mesh, PartitionSpec as P

MIRR = 62
LATE = 64
UNROLL = 8
ACCS = 8
CHUNK = 128
WINDOW = 1024


def sort_kernel(words_ref, out_ref):
    lists, rows, lanes = words_ref.shape
    row = lax.broadcasted_iota(jnp.int32, (rows, lanes), 0)
    lane = lax.broadcasted_iota(jnp.int32, (rows, lanes), 1)
    values = [words_ref[n] for n in range(lists)]

    def bit(distance):
        if distance < lanes:
            return (lane & distance) != 0
        return (row & (distance // lanes)) != 0

    size = 2
    while size <= rows * lanes:
        distance = size // 2
        while distance:
            high = bit(distance)
            keep_larger = high if size == rows * lanes else jnp.logical_xor(high, bit(size))
            axis, step = (1, distance) if distance < lanes else (0, distance // lanes)
            extent = (rows, lanes)[axis]
            for n, x in enumerate(values):
                other = jnp.where(
                    high, pltpu.roll(x, step, axis), pltpu.roll(x, extent - step, axis)
                )
                values[n] = jnp.where(keep_larger, jnp.maximum(x, other), jnp.minimum(x, other))
            distance //= 2
        size *= 2
    for n in range(lists):
        out_ref[n] = values[n]


def sort_lists(words):
    vmem = pl.BlockSpec(memory_space=pltpu.VMEM)
    return pl.pallas_call(
        sort_kernel,
        out_shape=jax.ShapeDtypeStruct(words.shape, words.dtype),
        in_specs=[vmem],
        out_specs=vmem,
        cost_estimate=pl.CostEstimate(
            flops=1000 * words.size, bytes_accessed=8 * words.size, transcendentals=0
        ),
        name="sort_lists",
    )(words)


def edge_kernel(bounds_ref, words_ref, table_ref, out_ref, words, table, *rest):
    accs, sems = rest[:-1], rest[-1]
    rows, width = table_ref.shape
    own = out_ref.shape[0]
    lists = sems.shape[0]
    length = words.shape[0] // lists

    def windows(m, act):
        def step(at, _):
            span = pl.ds(pl.multiple_of(m * length + at * WINDOW, WINDOW), WINDOW)
            act(pltpu.make_async_copy(words_ref.at[span], words.at[span], sems.at[m]))
            return 0

        last = (bounds_ref[1, m] + (WINDOW - 1)) // WINDOW
        lax.fori_loop(bounds_ref[0, m] // WINDOW, last, step, 0)

    for m in range(lists):
        windows(m, lambda copy: copy.start())

    def load(i, _):
        span = pl.ds(pl.multiple_of(i * CHUNK, CHUNK), CHUNK)
        table[span, :] = table_ref[span, :].astype(jnp.float32)
        return 0

    lax.fori_loop(0, rows // CHUNK, load, 0)

    def clear(i, _):
        span = pl.ds(pl.multiple_of(i * CHUNK, CHUNK), CHUNK)
        for acc in accs:
            acc[span, :] = jnp.zeros((CHUNK, width), jnp.float32)
        return 0

    lax.fori_loop(0, own // CHUNK, clear, 0)

    table_rows = table.reshape((rows, 1, width))
    acc_rows = [acc.reshape((own, 1, width)) for acc in accs]

    def add(base, count):
        takes, places = [], []
        for k in range(count):
            word = words[base + k]
            takes.append(word & 0xFFFF)
            places.append((word >> 16) & (own - 1))
        sums = [acc_rows[k][places[k]] + table_rows[takes[k]] for k in range(count)]
        for k in range(count):
            acc_rows[k][places[k]] = sums[k]

    for m in range(lists):
        windows(m, lambda copy: copy.wait())
        low, high = bounds_ref[0, m], bounds_ref[1, m]
        blocks = (high - low) // UNROLL

        def block(i, _):
            for group in range(UNROLL // ACCS):
                add(m * length + low + i * UNROLL + group * ACCS, ACCS)
            return 0

        def single(i, _):
            add(m * length + i, 1)
            return 0

        lax.fori_loop(0, blocks, block, 0)
        lax.fori_loop(low + blocks * UNROLL, high, single, 0)

    def store(i, _):
        span = pl.ds(pl.multiple_of(i * CHUNK, CHUNK), CHUNK)
        total = accs[0][span, :]
        for acc in accs[1:]:
            total = total + acc[span, :]
        out_ref[span, :] = total
        return 0

    lax.fori_loop(0, own // CHUNK, store, 0)


def edge_sums(bounds, words, table):
    rows, width = table.shape
    lists = bounds.shape[1]
    own = 2 * (rows // lists)
    vmem = pl.BlockSpec(memory_space=pltpu.VMEM)
    return pl.pallas_call(
        edge_kernel,
        out_shape=jax.ShapeDtypeStruct((own, width), jnp.float32),
        in_specs=[
            pl.BlockSpec(memory_space=pltpu.SMEM),
            pl.BlockSpec(memory_space=pl.ANY),
            vmem,
        ],
        out_specs=vmem,
        scratch_shapes=[
            pltpu.SMEM(words.shape, jnp.int32),
            pltpu.VMEM((rows, width), jnp.float32),
        ]
        + [pltpu.VMEM((own, width), jnp.float32)] * ACCS
        + [pltpu.SemaphoreType.DMA((lists,))],
        compiler_params=pltpu.CompilerParams(vmem_limit_bytes=40 * 1024 * 1024),
        cost_estimate=pl.CostEstimate(
            flops=16384 * width, bytes_accessed=4 * rows * width, transcendentals=0
        ),
        name="edge_sums",
    )(bounds, words, table)


def body(
    features,
    cotangent,
    edge_src,
    edge_dst,
    send_rows,
    recv_rows,
    in_degree,
    weight_self,
    weight_neigh,
):
    rows, width = features.shape
    half = width // 2
    early = rows - LATE
    dom_count = lax.axis_size("dom")
    member = ("y", "core")
    chips = lax.axis_size("y")
    members = 2 * chips
    core = lax.axis_index("core")
    chip = lax.axis_index("y")
    part_rows = rows * members
    contract_first = (((0,), (0,)), ((), ()))
    f32, bf16 = jnp.float32, jnp.bfloat16

    send_list = send_rows.reshape(-1)
    recv_list = recv_rows.reshape(-1)
    slot_count = send_list.shape[0]
    cap = slot_count // dom_count
    columns = lax.broadcasted_iota(jnp.int32, (slot_count, rows), 1)
    late_columns = lax.broadcasted_iota(jnp.int32, (slot_count, LATE), 1) + early
    pick_send = (send_list[:, None] == late_columns).astype(bf16)
    pick_recv = (recv_list[:, None] == columns).astype(bf16)
    is_mirror = lax.broadcasted_iota(jnp.int32, (rows, 1), 0) >= rows - MIRR
    late_mirror = is_mirror[early:]
    denominator = in_degree.reshape(-1).astype(f32)[:, None] + 1.0

    def over_dom(slots):
        return lax.all_to_all(slots, "dom", split_axis=0, concat_axis=0, tiled=True)

    def from_masters(values):
        slots = jnp.dot(pick_recv, values, preferred_element_type=f32).astype(bf16)
        return slots.reshape(dom_count, -1, values.shape[1])

    def at_mirrors(slots, values):
        arrived = lax.dot_general(
            pick_send, slots.reshape(slot_count, -1), contract_first, preferred_element_type=f32
        )
        return jnp.where(late_mirror, arrived.astype(bf16), values[early:])

    def over_member(blocks):
        return lax.all_to_all(blocks, member, split_axis=0, concat_axis=0, tiled=True)

    def gather(values):
        halves = jnp.stack([values[:, :half], values[:, half:]])
        every = jnp.broadcast_to(halves[None], (members // 2,) + halves.shape)
        return over_member(every.reshape(members, rows, half)).reshape(-1, half)

    def twin(values):
        return lax.ppermute(values, "core", [(0, 1), (1, 0)])

    def spread(values, combine):
        bit = chips // 2
        while bit:
            theirs = lax.ppermute(values, "y", [(y, y ^ bit) for y in range(chips)])
            values = combine(values, theirs)
            bit //= 2
        return combine(values, twin(values))

    def edge_lists(places, takes):
        words = jnp.where(places >= 0, (places << 16) | takes, part_rows << 16)
        words = sort_lists(words.reshape(2, -1, 128))
        words = spread(words, lambda mine, theirs: jnp.concatenate([mine, theirs], axis=1))
        lists = words.reshape(2, members, -1)
        bounds = jnp.stack(
            [
                jnp.sum((lists < (at * (2 * rows) << 16)).astype(jnp.int32), axis=2)
                for at in (chip, chip + 1)
            ],
            axis=1,
        )
        return [(bounds[n], words[n].reshape(-1)) for n in range(2)]

    def row_sums(lists, table):
        block = edge_sums(*lists, table)
        mine = lax.dynamic_slice_in_dim(block, core * rows, rows, 0)
        other = lax.dynamic_slice_in_dim(block, (1 - core) * rows, rows, 0)
        other = twin(other.astype(bf16)).astype(f32)
        return jnp.where(
            core == 0,
            jnp.concatenate([mine, other], axis=1),
            jnp.concatenate([other, mine], axis=1),
        )

    def mirror_slots(totals):
        slots = jnp.dot(pick_send, totals[early:].astype(bf16), preferred_element_type=f32)
        return slots.astype(bf16).reshape(dom_count, -1, width)

    def add_at_masters(slots):
        return lax.dot_general(
            pick_recv, slots.reshape(slot_count, width), contract_first, preferred_element_type=f32
        )

    slots, src, dst = lax.optimization_barrier((from_masters(features), edge_src, edge_dst))
    src, dst = src.reshape(1, -1), dst.reshape(1, -1)
    by_dst, by_src = edge_lists(jnp.concatenate([dst, src]), jnp.concatenate([src, dst]))
    late_rows = at_mirrors(over_dom(slots), features)
    table = gather(jnp.concatenate([features[:early], late_rows], axis=0))
    totals = row_sums(by_dst, table)
    totals = totals + add_at_masters(over_dom(mirror_slots(totals)))
    averaged = (totals / denominator).astype(bf16)

    pre = jnp.dot(features, weight_self, preferred_element_type=f32) + jnp.dot(
        averaged, weight_neigh, preferred_element_type=f32
    )
    gate_sig = jax.nn.sigmoid(pre)
    activated = (pre * gate_sig).astype(bf16)
    slope = gate_sig * (1.0 + pre * (1.0 - gate_sig))
    grad_pre = jnp.where(is_mirror, 0.0, cotangent.astype(f32) * slope).astype(bf16)
    grad_mean = (
        jnp.dot(grad_pre, weight_neigh.T, preferred_element_type=f32) / denominator
    ).astype(bf16)
    local_self = lax.dot_general(features, grad_pre, contract_first, preferred_element_type=f32)
    local_neigh = lax.dot_general(averaged, grad_pre, contract_first, preferred_element_type=f32)
    self_term = jnp.dot(grad_pre, weight_self.T, preferred_element_type=f32)

    local_weights = jnp.concatenate([local_self, local_neigh], axis=1).astype(bf16)
    share = local_weights.reshape(dom_count, -1, 2 * width)
    slots = from_masters(jnp.concatenate([grad_mean, activated], axis=1))
    moved = over_dom(jnp.concatenate([slots, share], axis=1))
    arrived = moved[:, :cap]
    late_rows = at_mirrors(arrived[:, :, :width], grad_mean)
    table = gather(jnp.concatenate([grad_mean[:early], late_rows], axis=0))
    activated_late = at_mirrors(arrived[:, :, width:], activated)
    activated = jnp.concatenate([activated[:early], activated_late], axis=0)

    weight_sum = spread(
        jnp.sum(moved[:, cap:].astype(f32), axis=0), lambda mine, theirs: mine + theirs
    )
    share = weight_sum.astype(bf16).reshape(-1, width)
    share = jnp.broadcast_to(share[None], (dom_count,) + share.shape)
    table, share = lax.optimization_barrier((table, share))
    totals = row_sums(by_src, table)
    moved = over_dom(jnp.concatenate([mirror_slots(totals), share], axis=1))
    weight_sums = moved[:, cap:].reshape(-1, 2 * width).astype(f32)
    back_sum = totals + add_at_masters(moved[:, :cap])
    grad_features = jnp.where(is_mirror, 0.0, back_sum + self_term).astype(bf16)
    return activated, grad_features, weight_sums[:, :width], weight_sums[:, width:]


def solution(mesh):
    devices = mesh.devices
    split = Mesh(
        devices.reshape(devices.shape[0], devices.shape[1] // 2, 2), ("dom", "y", "core")
    )
    every = ("dom", "y", "core")
    member = ("y", "core")
    placed = (
        P(every, None),
        P(every, None),
        P("dom", member, None),
        P("dom", member, None),
        P("dom", member, None, None),
        P("dom", member, None, None),
        P("dom", member, None),
        P(),
        P(),
    )
    return jax.shard_map(
        body,
        mesh=split,
        in_specs=placed,
        out_specs=(P(every, None), P(every, None), P(), P()),
        check_vma=False,
    )
```

```python
import jax
import jax.numpy as jnp
from jax import lax
from jax.experimental import pallas as pl
from jax.experimental.pallas import tpu as pltpu
from jax.sharding import Mesh, PartitionSpec as P

MIRR = 62
LATE = 64
UNROLL = 32
ACCS = 8
CHUNK = 128
WINDOW = 1024


def sort_kernel(words_ref, out_ref):
    lists, rows, lanes = words_ref.shape
    row = lax.broadcasted_iota(jnp.int32, (rows, lanes), 0)
    lane = lax.broadcasted_iota(jnp.int32, (rows, lanes), 1)
    values = [words_ref[n] for n in range(lists)]

    def bit(distance):
        if distance < lanes:
            return (lane & distance) != 0
        return (row & (distance // lanes)) != 0

    size = 2
    while size <= rows * lanes:
        distance = size // 2
        while distance:
            high = bit(distance)
            keep_larger = high if size == rows * lanes else jnp.logical_xor(high, bit(size))
            axis, step = (1, distance) if distance < lanes else (0, distance // lanes)
            extent = (rows, lanes)[axis]
            for n, x in enumerate(values):
                other = jnp.where(
                    high, pltpu.roll(x, step, axis), pltpu.roll(x, extent - step, axis)
                )
                values[n] = jnp.where(keep_larger, jnp.maximum(x, other), jnp.minimum(x, other))
            distance //= 2
        size *= 2
    for n in range(lists):
        out_ref[n] = values[n]


def sort_lists(words):
    vmem = pl.BlockSpec(memory_space=pltpu.VMEM)
    return pl.pallas_call(
        sort_kernel,
        out_shape=jax.ShapeDtypeStruct(words.shape, words.dtype),
        in_specs=[vmem],
        out_specs=vmem,
        cost_estimate=pl.CostEstimate(
            flops=1000 * words.size, bytes_accessed=8 * words.size, transcendentals=0
        ),
        name="sort_lists",
    )(words)


def edge_kernel(bounds_ref, words_ref, table_ref, out_ref, words, table, *rest):
    accs, sems = rest[:-1], rest[-1]
    rows, width = table.shape
    own = out_ref.shape[0]
    lists = sems.shape[0]
    length = words.shape[0] // lists

    def windows(m, act):
        def step(at, _):
            span = pl.ds(pl.multiple_of(m * length + at * WINDOW, WINDOW), WINDOW)
            act(pltpu.make_async_copy(words_ref.at[span], words.at[span], sems.at[m]))
            return 0

        last = (bounds_ref[1, m] + (WINDOW - 1)) // WINDOW
        lax.fori_loop(bounds_ref[0, m] // WINDOW, last, step, 0)

    for m in range(lists):
        windows(m, lambda copy: copy.start())

    def load(m, _):
        for at in range(0, rows // lists, CHUNK):
            span = pl.ds(pl.multiple_of(m * (rows // lists) + at, CHUNK), CHUNK)
            table[span, :] = table_ref[m, pl.ds(at, CHUNK), :].astype(jnp.float32)
        return 0

    lax.fori_loop(0, lists, load, 0)

    def clear(i, _):
        span = pl.ds(pl.multiple_of(i * CHUNK, CHUNK), CHUNK)
        for acc in accs:
            acc[span, :] = jnp.zeros((CHUNK, width), jnp.float32)
        return 0

    lax.fori_loop(0, own // CHUNK, clear, 0)

    table_rows = table.reshape((rows, 1, width))
    acc_rows = [acc.reshape((own, 1, width)) for acc in accs]

    def add(base, count):
        takes, places = [], []
        for k in range(count):
            word = words[base + k]
            takes.append(word & 0xFFFF)
            places.append((word >> 16) & (own - 1))
        sums = [acc_rows[k][places[k]] + table_rows[takes[k]] for k in range(count)]
        for k in range(count):
            acc_rows[k][places[k]] = sums[k]

    for m in range(lists):
        windows(m, lambda copy: copy.wait())
        low, high = bounds_ref[0, m], bounds_ref[1, m]
        done = low
        for count in (UNROLL, ACCS, 1):

            def block(i, _):
                for group in range(0, count, ACCS):
                    add(m * length + done + i * count + group, min(count, ACCS))
                return 0

            blocks = (high - done) // count
            lax.fori_loop(0, blocks, block, 0)
            done = done + blocks * count

    def store(i, _):
        span = pl.ds(pl.multiple_of(i * CHUNK, CHUNK), CHUNK)
        total = accs[0][span, :]
        for acc in accs[1:]:
            total = total + acc[span, :]
        out_ref[span, :] = total
        return 0

    lax.fori_loop(0, own // CHUNK, store, 0)


def edge_sums(bounds, words, table, own):
    lists, _, width = table.shape
    rows = lists * (own // 2)
    vmem = pl.BlockSpec(memory_space=pltpu.VMEM)
    return pl.pallas_call(
        edge_kernel,
        out_shape=jax.ShapeDtypeStruct((own, width), jnp.float32),
        in_specs=[
            pl.BlockSpec(memory_space=pltpu.SMEM),
            pl.BlockSpec(memory_space=pl.ANY),
            vmem,
        ],
        out_specs=vmem,
        scratch_shapes=[
            pltpu.SMEM(words.shape, jnp.int32),
            pltpu.VMEM((rows, width), jnp.float32),
        ]
        + [pltpu.VMEM((own, width), jnp.float32)] * ACCS
        + [pltpu.SemaphoreType.DMA((lists,))],
        compiler_params=pltpu.CompilerParams(vmem_limit_bytes=40 * 1024 * 1024),
        cost_estimate=pl.CostEstimate(
            flops=16384 * width, bytes_accessed=4 * rows * width, transcendentals=0
        ),
        name="edge_sums",
    )(bounds, words, table)


def body(
    features,
    cotangent,
    edge_src,
    edge_dst,
    send_rows,
    recv_rows,
    in_degree,
    weight_self,
    weight_neigh,
):
    rows, width = features.shape
    half = width // 2
    early = rows - LATE
    dom_count = lax.axis_size("dom")
    member = ("y", "core")
    chips = lax.axis_size("y")
    members = 2 * chips
    core = lax.axis_index("core")
    chip = lax.axis_index("y")
    part_rows = rows * members
    contract_first = (((0,), (0,)), ((), ()))
    f32, bf16 = jnp.float32, jnp.bfloat16

    send_list = send_rows.reshape(-1)
    recv_list = recv_rows.reshape(-1)
    slot_count = send_list.shape[0]
    cap = slot_count // dom_count
    columns = lax.broadcasted_iota(jnp.int32, (slot_count, rows), 1)
    late_columns = lax.broadcasted_iota(jnp.int32, (slot_count, LATE), 1) + early
    pick_send = (send_list[:, None] == late_columns).astype(bf16)
    pick_recv = (recv_list[:, None] == columns).astype(bf16)
    is_mirror = lax.broadcasted_iota(jnp.int32, (rows, 1), 0) >= rows - MIRR
    late_mirror = is_mirror[early:]
    denominator = in_degree.reshape(-1).astype(f32)[:, None] + 1.0

    def over_dom(slots):
        return lax.all_to_all(slots, "dom", split_axis=0, concat_axis=0, tiled=True)

    def from_masters(values):
        slots = jnp.dot(pick_recv, values, preferred_element_type=f32).astype(bf16)
        return slots.reshape(dom_count, -1, values.shape[1])

    def at_mirrors(slots, values):
        arrived = lax.dot_general(
            pick_send, slots.reshape(slot_count, -1), contract_first, preferred_element_type=f32
        )
        return jnp.where(late_mirror, arrived.astype(bf16), values[early:])

    def over_member(blocks):
        return lax.all_to_all(blocks, member, split_axis=0, concat_axis=0, tiled=True)

    def gather(values, share=None):
        halves = jnp.stack([values[:, :half], values[:, half:]])
        every = jnp.broadcast_to(halves[None], (members // 2,) + halves.shape)
        every = every.reshape(members, rows, half)
        if share is not None:
            share = jnp.broadcast_to(share[None], (members,) + share.shape)
            every = jnp.concatenate([every, share], axis=1)
        return over_member(every)

    def twin(values):
        return lax.ppermute(values, "core", [(0, 1), (1, 0)])

    def spread(values):
        bit = chips // 2
        while bit:
            theirs = lax.ppermute(values, "y", [(y, y ^ bit) for y in range(chips)])
            values = jnp.concatenate([values, theirs], axis=1)
            bit //= 2
        return jnp.concatenate([values, twin(values)], axis=1)

    def edge_lists(places, takes):
        words = jnp.where(places >= 0, (places << 16) | takes, part_rows << 16)
        words = spread(sort_lists(words.reshape(2, -1, 128)))
        lists = words.reshape(2, members, -1)
        bounds = jnp.stack(
            [
                jnp.sum((lists < (at * (2 * rows) << 16)).astype(jnp.int32), axis=2)
                for at in (chip, chip + 1)
            ],
            axis=1,
        )
        return [(bounds[n], words[n].reshape(-1)) for n in range(2)]

    def row_sums(lists, table):
        block = edge_sums(*lists, table, 2 * rows)
        mine = lax.dynamic_slice_in_dim(block, core * rows, rows, 0)
        other = lax.dynamic_slice_in_dim(block, (1 - core) * rows, rows, 0)
        other = twin(other.astype(bf16)).astype(f32)
        return jnp.where(
            core == 0,
            jnp.concatenate([mine, other], axis=1),
            jnp.concatenate([other, mine], axis=1),
        )

    def mirror_slots(totals):
        slots = jnp.dot(pick_send, totals[early:].astype(bf16), preferred_element_type=f32)
        return slots.astype(bf16).reshape(dom_count, -1, width)

    def add_at_masters(slots):
        return lax.dot_general(
            pick_recv, slots.reshape(slot_count, width), contract_first, preferred_element_type=f32
        )

    slots, src, dst = lax.optimization_barrier((from_masters(features), edge_src, edge_dst))
    src, dst = src.reshape(1, -1), dst.reshape(1, -1)
    by_dst, by_src = edge_lists(jnp.concatenate([dst, src]), jnp.concatenate([src, dst]))
    late_rows = at_mirrors(over_dom(slots), features)
    table = gather(jnp.concatenate([features[:early], late_rows], axis=0))
    totals = row_sums(by_dst, table)
    totals = totals + add_at_masters(over_dom(mirror_slots(totals)))
    averaged = (totals / denominator).astype(bf16)

    pre = jnp.dot(features, weight_self, preferred_element_type=f32) + jnp.dot(
        averaged, weight_neigh, preferred_element_type=f32
    )
    gate_sig = jax.nn.sigmoid(pre)
    activated = (pre * gate_sig).astype(bf16)
    slope = gate_sig * (1.0 + pre * (1.0 - gate_sig))
    grad_pre = jnp.where(is_mirror, 0.0, cotangent.astype(f32) * slope).astype(bf16)
    grad_mean = (
        jnp.dot(grad_pre, weight_neigh.T, preferred_element_type=f32) / denominator
    ).astype(bf16)
    local_self = lax.dot_general(features, grad_pre, contract_first, preferred_element_type=f32)
    local_neigh = lax.dot_general(averaged, grad_pre, contract_first, preferred_element_type=f32)
    self_term = jnp.dot(grad_pre, weight_self.T, preferred_element_type=f32)

    local_weights = jnp.concatenate([local_self, local_neigh], axis=1).astype(bf16)
    share = local_weights.reshape(dom_count, -1, 2 * width)
    slots = from_masters(jnp.concatenate([grad_mean, activated], axis=1))
    moved = over_dom(jnp.concatenate([slots, share], axis=1))
    arrived = moved[:, :cap]
    late_rows = at_mirrors(arrived[:, :, :width], grad_mean)
    share = jnp.sum(moved[:, cap:].astype(f32), axis=0).astype(bf16).reshape(-1, half)
    table = gather(jnp.concatenate([grad_mean[:early], late_rows], axis=0), share)
    activated_late = at_mirrors(arrived[:, :, width:], activated)
    activated = jnp.concatenate([activated[:early], activated_late], axis=0)

    share = jnp.sum(table[:, rows:].astype(f32), axis=0).astype(bf16).reshape(-1, width)
    share = jnp.broadcast_to(share[None], (dom_count,) + share.shape)
    totals = row_sums(by_src, table)
    moved = over_dom(jnp.concatenate([mirror_slots(totals), share], axis=1))
    weight_sums = moved[:, cap:].reshape(-1, 2 * width).astype(f32)
    back_sum = totals + add_at_masters(moved[:, :cap])
    grad_features = jnp.where(is_mirror, 0.0, back_sum + self_term).astype(bf16)
    return activated, grad_features, weight_sums[:, :width], weight_sums[:, width:]


def solution(mesh):
    devices = mesh.devices
    split = Mesh(
        devices.reshape(devices.shape[0], devices.shape[1] // 2, 2), ("dom", "y", "core")
    )
    every = ("dom", "y", "core")
    member = ("y", "core")
    placed = (
        P(every, None),
        P(every, None),
        P("dom", member, None),
        P("dom", member, None),
        P("dom", member, None, None),
        P("dom", member, None, None),
        P("dom", member, None),
        P(),
        P(),
    )
    return jax.shard_map(
        body,
        mesh=split,
        in_specs=placed,
        out_specs=(P(every, None), P(every, None), P(), P()),
        check_vma=False,
    )
```

```python
import jax
import jax.numpy as jnp
from jax import lax
from jax.experimental import pallas as pl
from jax.experimental.pallas import tpu as pltpu
from jax.sharding import Mesh, PartitionSpec as P

MIRR = 62
LATE = 64
UNROLL = 32
ACCS = 8
CHUNK = 128
WINDOW = 1024


def sort_kernel(words_ref, out_ref):
    lists, rows, lanes = words_ref.shape
    row = lax.broadcasted_iota(jnp.int32, (rows, lanes), 0)
    lane = lax.broadcasted_iota(jnp.int32, (rows, lanes), 1)
    values = [words_ref[n] for n in range(lists)]

    def bit(distance):
        if distance < lanes:
            return (lane & distance) != 0
        return (row & (distance // lanes)) != 0

    size = 2
    while size <= rows * lanes:
        distance = size // 2
        while distance:
            high = bit(distance)
            keep_larger = high if size == rows * lanes else jnp.logical_xor(high, bit(size))
            axis, step = (1, distance) if distance < lanes else (0, distance // lanes)
            extent = (rows, lanes)[axis]
            for n, x in enumerate(values):
                other = jnp.where(
                    high, pltpu.roll(x, step, axis), pltpu.roll(x, extent - step, axis)
                )
                values[n] = jnp.where(keep_larger, jnp.maximum(x, other), jnp.minimum(x, other))
            distance //= 2
        size *= 2
    for n in range(lists):
        out_ref[n] = values[n]


def sort_lists(words):
    vmem = pl.BlockSpec(memory_space=pltpu.VMEM)
    return pl.pallas_call(
        sort_kernel,
        out_shape=jax.ShapeDtypeStruct(words.shape, words.dtype),
        in_specs=[vmem],
        out_specs=vmem,
        cost_estimate=pl.CostEstimate(
            flops=1000 * words.size, bytes_accessed=8 * words.size, transcendentals=0
        ),
        name="sort_lists",
    )(words)


def edge_kernel(bounds_ref, words_ref, table_ref, out_ref, words, table, *rest):
    accs, sems = rest[:-1], rest[-1]
    rows, width = table.shape
    own = out_ref.shape[0]
    lists = sems.shape[0]
    length = words.shape[0] // lists

    def windows(m, act):
        def step(at, _):
            span = pl.ds(pl.multiple_of(m * length + at * WINDOW, WINDOW), WINDOW)
            act(pltpu.make_async_copy(words_ref.at[span], words.at[span], sems.at[m]))
            return 0

        last = (bounds_ref[1, m] + (WINDOW - 1)) // WINDOW
        lax.fori_loop(bounds_ref[0, m] // WINDOW, last, step, 0)

    for m in range(lists):
        windows(m, lambda copy: copy.start())

    def load(m, _):
        for at in range(0, rows // lists, CHUNK):
            span = pl.ds(pl.multiple_of(m * (rows // lists) + at, CHUNK), CHUNK)
            table[span, :] = table_ref[m, pl.ds(at, CHUNK), :].astype(jnp.float32)
        return 0

    lax.fori_loop(0, lists, load, 0)

    def clear(i, _):
        span = pl.ds(pl.multiple_of(i * CHUNK, CHUNK), CHUNK)
        for acc in accs:
            acc[span, :] = jnp.zeros((CHUNK, width), jnp.float32)
        return 0

    lax.fori_loop(0, own // CHUNK, clear, 0)

    table_rows = table.reshape((rows, 1, width))
    acc_rows = [acc.reshape((own, 1, width)) for acc in accs]

    def add(base, count):
        takes, places = [], []
        for k in range(count):
            word = words[base + k]
            takes.append(word & 0xFFFF)
            places.append(word >> 16)
        sums = [acc_rows[k][places[k]] + table_rows[takes[k]] for k in range(count)]
        for k in range(count):
            acc_rows[k][places[k]] = sums[k]

    for m in range(lists):
        windows(m, lambda copy: copy.wait())
        low, high = bounds_ref[0, m], bounds_ref[1, m]
        done = low
        for count in (UNROLL, ACCS, 1):

            def block(i, _):
                for group in range(0, count, ACCS):
                    add(m * length + done + i * count + group, min(count, ACCS))
                return 0

            blocks = (high - done) // count
            lax.fori_loop(0, blocks, block, 0)
            done = done + blocks * count

    def store(i, _):
        span = pl.ds(pl.multiple_of(i * CHUNK, CHUNK), CHUNK)
        total = accs[0][span, :]
        for acc in accs[1:]:
            total = total + acc[span, :]
        out_ref[span, :] = total
        return 0

    lax.fori_loop(0, own // CHUNK, store, 0)


def edge_sums(bounds, words, table, own):
    lists, _, width = table.shape
    rows = lists * (own // 2)
    vmem = pl.BlockSpec(memory_space=pltpu.VMEM)
    return pl.pallas_call(
        edge_kernel,
        out_shape=jax.ShapeDtypeStruct((own, width), jnp.float32),
        in_specs=[
            pl.BlockSpec(memory_space=pltpu.SMEM),
            pl.BlockSpec(memory_space=pl.ANY),
            vmem,
        ],
        out_specs=vmem,
        scratch_shapes=[
            pltpu.SMEM(words.shape, jnp.int32),
            pltpu.VMEM((rows, width), jnp.float32),
        ]
        + [pltpu.VMEM((own, width), jnp.float32)] * ACCS
        + [pltpu.SemaphoreType.DMA((lists,))],
        compiler_params=pltpu.CompilerParams(vmem_limit_bytes=40 * 1024 * 1024),
        cost_estimate=pl.CostEstimate(
            flops=16384 * width, bytes_accessed=4 * rows * width, transcendentals=0
        ),
        name="edge_sums",
    )(bounds, words, table)


def body(
    features,
    cotangent,
    edge_src,
    edge_dst,
    send_rows,
    recv_rows,
    in_degree,
    weight_self,
    weight_neigh,
):
    rows, width = features.shape
    half = width // 2
    early = rows - LATE
    dom_count = lax.axis_size("dom")
    member = ("y", "core")
    chips = lax.axis_size("y")
    members = 2 * chips
    core = lax.axis_index("core")
    chip = lax.axis_index("y")
    part_rows = rows * members
    contract_first = (((0,), (0,)), ((), ()))
    f32, bf16 = jnp.float32, jnp.bfloat16

    send_list = send_rows.reshape(-1)
    recv_list = recv_rows.reshape(-1)
    slot_count = send_list.shape[0]
    cap = slot_count // dom_count
    columns = lax.broadcasted_iota(jnp.int32, (slot_count, rows), 1)
    late_columns = lax.broadcasted_iota(jnp.int32, (slot_count, LATE), 1) + early
    pick_send = (send_list[:, None] == late_columns).astype(bf16)
    pick_recv = (recv_list[:, None] == columns).astype(bf16)
    is_mirror = lax.broadcasted_iota(jnp.int32, (rows, 1), 0) >= rows - MIRR
    late_mirror = is_mirror[early:]
    denominator = in_degree.reshape(-1).astype(f32)[:, None] + 1.0

    def over_dom(slots):
        return lax.all_to_all(slots, "dom", split_axis=0, concat_axis=0, tiled=True)

    def from_masters(values):
        slots = jnp.dot(pick_recv, values, preferred_element_type=f32).astype(bf16)
        return slots.reshape(dom_count, -1, values.shape[1])

    def at_mirrors(slots, values):
        arrived = lax.dot_general(
            pick_send, slots.reshape(slot_count, -1), contract_first, preferred_element_type=f32
        )
        return jnp.where(late_mirror, arrived.astype(bf16), values[early:])

    def over_member(blocks):
        return lax.all_to_all(blocks, member, split_axis=0, concat_axis=0, tiled=True)

    def copies(values, share=None):
        halves = jnp.stack([values[:, :half], values[:, half:]])
        every = jnp.broadcast_to(halves[None], (members // 2,) + halves.shape)
        every = every.reshape(members, rows, half)
        if share is not None:
            share = jnp.broadcast_to(share[None], (members,) + share.shape)
            every = jnp.concatenate([every, share], axis=1)
        return every

    def twin(values):
        return lax.ppermute(values, "core", [(0, 1), (1, 0)])

    def with_theirs(words, bit):
        theirs = lax.ppermute(words, "y", [(y, y ^ bit) for y in range(chips)])
        return jnp.concatenate([words, theirs], axis=1)

    def own_lists(places, takes):
        words = jnp.where(places >= 0, (places << 16) | takes, part_rows << 16)
        return sort_lists(words.reshape(2, -1, 128))

    def runs(words):
        lists = words.reshape(2, members, -1)
        bounds = jnp.stack(
            [
                jnp.sum((lists < (at * (2 * rows) << 16)).astype(jnp.int32), axis=2)
                for at in (chip, chip + 1)
            ],
            axis=1,
        )
        words = words & ((2 * rows - 1) << 16 | 0xFFFF)
        return [(bounds[n], words[n].reshape(-1)) for n in range(2)]

    def row_sums(lists, table):
        block = edge_sums(*lists, table, 2 * rows)
        mine = lax.dynamic_slice_in_dim(block, core * rows, rows, 0)
        other = lax.dynamic_slice_in_dim(block, (1 - core) * rows, rows, 0)
        other = twin(other.astype(bf16)).astype(f32)
        return jnp.where(
            core == 0,
            jnp.concatenate([mine, other], axis=1),
            jnp.concatenate([other, mine], axis=1),
        )

    def mirror_slots(totals):
        slots = jnp.dot(pick_send, totals[early:].astype(bf16), preferred_element_type=f32)
        return slots.astype(bf16).reshape(dom_count, -1, width)

    def add_at_masters(slots):
        return lax.dot_general(
            pick_recv, slots.reshape(slot_count, width), contract_first, preferred_element_type=f32
        )

    slots, src, dst = lax.optimization_barrier((from_masters(features), edge_src, edge_dst))
    src, dst = src.reshape(1, -1), dst.reshape(1, -1)
    words = own_lists(jnp.concatenate([dst, src]), jnp.concatenate([src, dst]))
    bit = chips // 2
    while bit > 1:
        words = with_theirs(words, bit)
        bit //= 2
    late_rows = at_mirrors(over_dom(slots), features)
    every = copies(jnp.concatenate([features[:early], late_rows], axis=0))
    every, words = lax.optimization_barrier((every, words))
    table = over_member(every)
    words = with_theirs(words, 1)
    by_dst, by_src = runs(jnp.concatenate([words, twin(words)], axis=1))
    totals = row_sums(by_dst, table)
    totals = totals + add_at_masters(over_dom(mirror_slots(totals)))
    averaged = (totals / denominator).astype(bf16)

    pre = jnp.dot(features, weight_self, preferred_element_type=f32) + jnp.dot(
        averaged, weight_neigh, preferred_element_type=f32
    )
    gate_sig = jax.nn.sigmoid(pre)
    activated = (pre * gate_sig).astype(bf16)
    slope = gate_sig * (1.0 + pre * (1.0 - gate_sig))
    grad_pre = jnp.where(is_mirror, 0.0, cotangent.astype(f32) * slope).astype(bf16)
    grad_mean = (
        jnp.dot(grad_pre, weight_neigh.T, preferred_element_type=f32) / denominator
    ).astype(bf16)
    local_self = lax.dot_general(features, grad_pre, contract_first, preferred_element_type=f32)
    local_neigh = lax.dot_general(averaged, grad_pre, contract_first, preferred_element_type=f32)
    self_term = jnp.dot(grad_pre, weight_self.T, preferred_element_type=f32)

    local_weights = jnp.concatenate([local_self, local_neigh], axis=1).astype(bf16)
    share = local_weights.reshape(dom_count, -1, 2 * width)
    slots = from_masters(jnp.concatenate([grad_mean, activated], axis=1))
    moved = over_dom(jnp.concatenate([slots, share], axis=1))
    arrived = moved[:, :cap]
    late_rows = at_mirrors(arrived[:, :, :width], grad_mean)
    share = jnp.sum(moved[:, cap:].astype(f32), axis=0).astype(bf16).reshape(-1, half)
    table = over_member(copies(jnp.concatenate([grad_mean[:early], late_rows], axis=0), share))
    activated_late = at_mirrors(arrived[:, :, width:], activated)
    activated = jnp.concatenate([activated[:early], activated_late], axis=0)

    share = jnp.sum(table[:, rows:].astype(f32), axis=0).astype(bf16).reshape(-1, width)
    share = jnp.broadcast_to(share[None], (dom_count,) + share.shape)
    totals = row_sums(by_src, table)
    moved = over_dom(jnp.concatenate([mirror_slots(totals), share], axis=1))
    weight_sums = moved[:, cap:].reshape(-1, 2 * width).astype(f32)
    back_sum = totals + add_at_masters(moved[:, :cap])
    grad_features = jnp.where(is_mirror, 0.0, back_sum + self_term).astype(bf16)
    return activated, grad_features, weight_sums[:, :width], weight_sums[:, width:]


def solution(mesh):
    devices = mesh.devices
    split = Mesh(
        devices.reshape(devices.shape[0], devices.shape[1] // 2, 2), ("dom", "y", "core")
    )
    every = ("dom", "y", "core")
    member = ("y", "core")
    placed = (
        P(every, None),
        P(every, None),
        P("dom", member, None),
        P("dom", member, None),
        P("dom", member, None, None),
        P("dom", member, None, None),
        P("dom", member, None),
        P(),
        P(),
    )
    return jax.shard_map(
        body,
        mesh=split,
        in_specs=placed,
        out_specs=(P(every, None), P(every, None), P(), P()),
        check_vma=False,
    )
```

```python
import jax
import jax.numpy as jnp
from jax import lax
from jax.experimental import pallas as pl
from jax.experimental.pallas import tpu as pltpu
from jax.sharding import Mesh, PartitionSpec as P

MIRR = 62
LATE = 64
UNROLL = 32
ACCS = 8
CHUNK = 128
WINDOW = 1024


def sort_kernel(words_ref, out_ref):
    lists, rows, lanes = words_ref.shape
    row = lax.broadcasted_iota(jnp.int32, (rows, lanes), 0)
    lane = lax.broadcasted_iota(jnp.int32, (rows, lanes), 1)
    values = [words_ref[n] for n in range(lists)]

    def bit(distance):
        if distance < lanes:
            return (lane & distance) != 0
        return (row & (distance // lanes)) != 0

    size = 2
    while size <= rows * lanes:
        distance = size // 2
        while distance:
            high = bit(distance)
            keep_larger = high if size == rows * lanes else jnp.logical_xor(high, bit(size))
            axis, step = (1, distance) if distance < lanes else (0, distance // lanes)
            extent = (rows, lanes)[axis]
            for n, x in enumerate(values):
                other = jnp.where(
                    high, pltpu.roll(x, step, axis), pltpu.roll(x, extent - step, axis)
                )
                values[n] = jnp.where(keep_larger, jnp.maximum(x, other), jnp.minimum(x, other))
            distance //= 2
        size *= 2
    for n in range(lists):
        out_ref[n] = values[n]


def sort_lists(words):
    vmem = pl.BlockSpec(memory_space=pltpu.VMEM)
    return pl.pallas_call(
        sort_kernel,
        out_shape=jax.ShapeDtypeStruct(words.shape, words.dtype),
        in_specs=[vmem],
        out_specs=vmem,
        cost_estimate=pl.CostEstimate(
            flops=1000 * words.size, bytes_accessed=8 * words.size, transcendentals=0
        ),
        name="sort_lists",
    )(words)


def edge_kernel(bounds_ref, words_ref, table_ref, out_ref, words, table, *rest):
    accs, sems = rest[:-1], rest[-1]
    rows, width = table.shape
    own = out_ref.shape[0]
    lists = sems.shape[0]
    length = words.shape[0] // lists

    def windows(m, act):
        def step(at, _):
            span = pl.ds(pl.multiple_of(m * length + at * WINDOW, WINDOW), WINDOW)
            act(pltpu.make_async_copy(words_ref.at[span], words.at[span], sems.at[m]))
            return 0

        last = (bounds_ref[1, m] + (WINDOW - 1)) // WINDOW
        lax.fori_loop(bounds_ref[0, m] // WINDOW, last, step, 0)

    for m in range(lists):
        windows(m, lambda copy: copy.start())

    def load(m, _):
        for at in range(0, rows // lists, CHUNK):
            span = pl.ds(pl.multiple_of(m * (rows // lists) + at, CHUNK), CHUNK)
            table[span, :] = table_ref[m, pl.ds(at, CHUNK), :].astype(jnp.float32)
        return 0

    lax.fori_loop(0, lists, load, 0)

    def clear(i, _):
        span = pl.ds(pl.multiple_of(i * CHUNK, CHUNK), CHUNK)
        for acc in accs:
            acc[span, :] = jnp.zeros((CHUNK, width), jnp.float32)
        return 0

    lax.fori_loop(0, own // CHUNK, clear, 0)

    table_rows = table.reshape((rows, 1, width))
    acc_rows = [acc.reshape((own, 1, width)) for acc in accs]

    def add(base, count):
        takes, places = [], []
        for k in range(count):
            word = words[base + k]
            takes.append(word & 0xFFFF)
            places.append(word >> 16)
        sums = [acc_rows[k][places[k]] + table_rows[takes[k]] for k in range(count)]
        for k in range(count):
            acc_rows[k][places[k]] = sums[k]

    for m in range(lists):
        windows(m, lambda copy: copy.wait())
        low, high = bounds_ref[0, m], bounds_ref[1, m]
        done = low
        for count in (UNROLL, ACCS, 1):

            def block(i, _):
                for group in range(0, count, ACCS):
                    add(m * length + done + i * count + group, min(count, ACCS))
                return 0

            blocks = (high - done) // count
            lax.fori_loop(0, blocks, block, 0)
            done = done + blocks * count

    def store(i, _):
        span = pl.ds(pl.multiple_of(i * CHUNK, CHUNK), CHUNK)
        total = accs[0][span, :]
        for acc in accs[1:]:
            total = total + acc[span, :]
        out_ref[span, :] = total
        return 0

    lax.fori_loop(0, own // CHUNK, store, 0)


def edge_sums(bounds, words, table, own):
    lists, _, width = table.shape
    rows = lists * (own // 2)
    vmem = pl.BlockSpec(memory_space=pltpu.VMEM)
    return pl.pallas_call(
        edge_kernel,
        out_shape=jax.ShapeDtypeStruct((own, width), jnp.float32),
        in_specs=[
            pl.BlockSpec(memory_space=pltpu.SMEM),
            pl.BlockSpec(memory_space=pl.ANY),
            vmem,
        ],
        out_specs=vmem,
        scratch_shapes=[
            pltpu.SMEM(words.shape, jnp.int32),
            pltpu.VMEM((rows, width), jnp.float32),
        ]
        + [pltpu.VMEM((own, width), jnp.float32)] * ACCS
        + [pltpu.SemaphoreType.DMA((lists,))],
        compiler_params=pltpu.CompilerParams(vmem_limit_bytes=40 * 1024 * 1024),
        cost_estimate=pl.CostEstimate(
            flops=16384 * width, bytes_accessed=4 * rows * width, transcendentals=0
        ),
        name="edge_sums",
    )(bounds, words, table)


def body(
    features,
    cotangent,
    edge_src,
    edge_dst,
    send_rows,
    recv_rows,
    in_degree,
    weight_self,
    weight_neigh,
):
    rows, width = features.shape
    half = width // 2
    early = rows - LATE
    dom_count = lax.axis_size("dom")
    member = ("y", "core")
    chips = lax.axis_size("y")
    members = 2 * chips
    core = lax.axis_index("core")
    chip = lax.axis_index("y")
    part_rows = rows * members
    contract_first = (((0,), (0,)), ((), ()))
    f32, bf16 = jnp.float32, jnp.bfloat16

    send_list = send_rows.reshape(-1)
    recv_list = recv_rows.reshape(-1)
    slot_count = send_list.shape[0]
    cap = slot_count // dom_count
    columns = lax.broadcasted_iota(jnp.int32, (slot_count, rows), 1)
    late_columns = lax.broadcasted_iota(jnp.int32, (slot_count, LATE), 1) + early
    pick_send = (send_list[:, None] == late_columns).astype(bf16)
    pick_recv = (recv_list[:, None] == columns).astype(bf16)
    is_mirror = lax.broadcasted_iota(jnp.int32, (rows, 1), 0) >= rows - MIRR
    late_mirror = is_mirror[early:]
    denominator = in_degree.reshape(-1).astype(f32)[:, None] + 1.0

    def over_dom(slots):
        return lax.all_to_all(slots, "dom", split_axis=0, concat_axis=0, tiled=True)

    def from_masters(values):
        slots = jnp.dot(pick_recv, values, preferred_element_type=f32).astype(bf16)
        return slots.reshape(dom_count, -1, values.shape[1])

    def at_mirrors(slots, values):
        arrived = lax.dot_general(
            pick_send, slots.reshape(slot_count, -1), contract_first, preferred_element_type=f32
        )
        return jnp.where(late_mirror, arrived.astype(bf16), values[early:])

    def over_member(blocks):
        return lax.all_to_all(blocks, member, split_axis=0, concat_axis=0, tiled=True)

    def copies(values, share=None):
        halves = jnp.stack([values[:, :half], values[:, half:]])
        every = jnp.broadcast_to(halves[None], (members // 2,) + halves.shape)
        every = every.reshape(members, rows, half)
        if share is not None:
            share = jnp.broadcast_to(share[None], (members,) + share.shape)
            every = jnp.concatenate([every, share], axis=1)
        return every

    def twin(values):
        return lax.ppermute(values, "core", [(0, 1), (1, 0)])

    def with_theirs(words, bit):
        theirs = lax.ppermute(words, "y", [(y, y ^ bit) for y in range(chips)])
        return jnp.concatenate([words, theirs], axis=1)

    def own_lists(places, takes):
        words = jnp.where(places >= 0, (places << 16) | takes, part_rows << 16)
        return sort_lists(words.reshape(2, -1, 128))

    def runs(words):
        lists = words.reshape(2, members, -1)
        bounds = jnp.stack(
            [
                jnp.sum((lists < (at * (2 * rows) << 16)).astype(jnp.int32), axis=2)
                for at in (chip, chip + 1)
            ],
            axis=1,
        )
        words = words & ((2 * rows - 1) << 16 | 0xFFFF)
        return [(bounds[n], words[n].reshape(-1)) for n in range(2)]

    def row_sums(lists, table):
        block = edge_sums(*lists, table, 2 * rows)
        mine = lax.dynamic_slice_in_dim(block, core * rows, rows, 0)
        other = lax.dynamic_slice_in_dim(block, (1 - core) * rows, rows, 0)
        other = twin(other.astype(bf16)).astype(f32)
        return jnp.where(
            core == 0,
            jnp.concatenate([mine, other], axis=1),
            jnp.concatenate([other, mine], axis=1),
        )

    def mirror_slots(totals):
        slots = jnp.dot(pick_send, totals[early:].astype(bf16), preferred_element_type=f32)
        return slots.astype(bf16).reshape(dom_count, -1, width)

    def add_at_masters(slots):
        return lax.dot_general(
            pick_recv, slots.reshape(slot_count, width), contract_first, preferred_element_type=f32
        )

    slots, src, dst = lax.optimization_barrier((from_masters(features), edge_src, edge_dst))
    src, dst = src.reshape(1, -1), dst.reshape(1, -1)
    words = own_lists(jnp.concatenate([dst, src]), jnp.concatenate([src, dst]))
    bit = chips // 2
    while bit > 1:
        words = with_theirs(words, bit)
        bit //= 2
    late_rows = at_mirrors(over_dom(slots), features)
    every = copies(jnp.concatenate([features[:early], late_rows], axis=0))
    every, words = lax.optimization_barrier((every, words))
    table = over_member(every)
    words, table = lax.optimization_barrier((with_theirs(words, 1), table))
    by_dst, by_src = runs(jnp.concatenate([words, twin(words)], axis=1))
    totals = row_sums(by_dst, table)
    totals = totals + add_at_masters(over_dom(mirror_slots(totals)))
    averaged = (totals / denominator).astype(bf16)

    pre = jnp.dot(features, weight_self, preferred_element_type=f32) + jnp.dot(
        averaged, weight_neigh, preferred_element_type=f32
    )
    gate_sig = jax.nn.sigmoid(pre)
    activated = (pre * gate_sig).astype(bf16)
    slope = gate_sig * (1.0 + pre * (1.0 - gate_sig))
    grad_pre = jnp.where(is_mirror, 0.0, cotangent.astype(f32) * slope).astype(bf16)
    grad_mean = (
        jnp.dot(grad_pre, weight_neigh.T, preferred_element_type=f32) / denominator
    ).astype(bf16)
    local_self = lax.dot_general(features, grad_pre, contract_first, preferred_element_type=f32)
    local_neigh = lax.dot_general(averaged, grad_pre, contract_first, preferred_element_type=f32)
    self_term = jnp.dot(grad_pre, weight_self.T, preferred_element_type=f32)

    local_weights = jnp.concatenate([local_self, local_neigh], axis=1).astype(bf16)
    share = local_weights.reshape(dom_count, -1, 2 * width)
    slots = from_masters(jnp.concatenate([grad_mean, activated], axis=1))
    moved = over_dom(jnp.concatenate([slots, share], axis=1))
    arrived = moved[:, :cap]
    late_rows = at_mirrors(arrived[:, :, :width], grad_mean)
    share = jnp.sum(moved[:, cap:].astype(f32), axis=0).astype(bf16).reshape(-1, half)
    table = over_member(copies(jnp.concatenate([grad_mean[:early], late_rows], axis=0), share))
    activated_late = at_mirrors(arrived[:, :, width:], activated)
    activated = jnp.concatenate([activated[:early], activated_late], axis=0)

    share = jnp.sum(table[:, rows:].astype(f32), axis=0).astype(bf16).reshape(-1, width)
    share = jnp.broadcast_to(share[None], (dom_count,) + share.shape)
    totals = row_sums(by_src, table)
    moved = over_dom(jnp.concatenate([mirror_slots(totals), share], axis=1))
    weight_sums = moved[:, cap:].reshape(-1, 2 * width).astype(f32)
    back_sum = totals + add_at_masters(moved[:, :cap])
    grad_features = jnp.where(is_mirror, 0.0, back_sum + self_term).astype(bf16)
    return activated, grad_features, weight_sums[:, :width], weight_sums[:, width:]


def solution(mesh):
    devices = mesh.devices
    split = Mesh(
        devices.reshape(devices.shape[0], devices.shape[1] // 2, 2), ("dom", "y", "core")
    )
    every = ("dom", "y", "core")
    member = ("y", "core")
    placed = (
        P(every, None),
        P(every, None),
        P("dom", member, None),
        P("dom", member, None),
        P("dom", member, None, None),
        P("dom", member, None, None),
        P("dom", member, None),
        P(),
        P(),
    )
    return jax.shard_map(
        body,
        mesh=split,
        in_specs=placed,
        out_specs=(P(every, None), P(every, None), P(), P()),
        check_vma=False,
    )
```
